128 devices in a mesh: tm: 2 (over core), blk: 64 (over z, y, x).
Axes of the slice: x: 4, y: 4, z: 4, core: 2. Of those that a mesh axis runs over, the one named last changes fastest.
Arguments:
- edge_prec: float32 [4, 1024, 1024], P('tm', 'blk'), may hold values from -2 to 10, as said below
- nugget: float32 [4, 1024], P('tm', 'blk'), may hold values from 0.05 to 0.5
- arrow: float32 [16, 4, 1024], P(None, 'tm', 'blk'), may hold values from -0.09375 to 0.09375
- fixed_prec: float32 [16, 16], replicated, may hold values from -1 to 6, as said below
- rhs_latent: float32 [4, 1024], P('tm', 'blk'), may hold values from -6 to 6
- rhs_fixed: float32 [16], replicated, may hold values from -6 to 6
Outputs:
- latent_sol: float32 [4, 1024], P('tm', 'blk')
- fixed_sol: float32 [16], replicated
The draws below stay inside these ranges and needn't reach their ends.
Inputs may be any that keep to these rules, and one draw needn't show every extreme that they name: Every edge_prec[k] is symmetric positive definite. fixed_prec is symmetric, and the whole arrowhead matrix of the steps is positive definite.
All inputs are finite; a program needn't handle non-finite values.
Results may differ from the reference program's by a relative error of at most 0.0003.
Values sent between devices are 32-bit elements; how exact they have to be, the bound alone decides.
A program may use at most 192 MiB of HBM per device.

```python
import math
import jax
import jax.numpy as jnp
from jax import lax

NODES = 1024
FIXED = 16
BLOCKS = 4


def draw_edge_prec(key, part):
    key = jax.random.fold_in(key, 11)
    key_noise, key_diag, key_level = jax.random.split(key, 3)
    noise = jnp.clip(jax.random.normal(key_noise, (BLOCKS, NODES, NODES), jnp.float32), -3.0, 3.0)
    diag_values = jax.random.uniform(key_diag, (BLOCKS, NODES), jnp.float32, 2.6, 5.0)
    scaling = jnp.exp(jax.random.uniform(key_level, (BLOCKS,), jnp.float32, -0.6931472, 0.6931472))
    symmetric = (noise + jnp.swapaxes(noise, 1, 2)) * (0.70710678 / math.sqrt(NODES))
    identity = jnp.eye(NODES, dtype=jnp.float32)
    whole = symmetric * (1.0 - identity) + identity[None] * diag_values[:, :, None]
    return whole * scaling[:, None, None]


def draw_fixed_prec(key, part):
    key = jax.random.fold_in(key, 23)
    key_noise, key_diag = jax.random.split(key, 2)
    noise = jnp.clip(jax.random.normal(key_noise, (FIXED, FIXED), jnp.float32), -3.0, 3.0)
    diag_values = jax.random.uniform(key_diag, (FIXED,), jnp.float32, 3.0, 6.0)
    symmetric = (noise + noise.T) * (0.35355339 / math.sqrt(FIXED))
    identity = jnp.eye(FIXED, dtype=jnp.float32)
    return symmetric * (1.0 - identity) + identity * diag_values[None, :]


def steps_of(stream_key, extent, cuts, low, high):
    def one(axis_at, parts):
        draws = jax.random.uniform(jax.random.fold_in(jax.random.fold_in(stream_key, 6), axis_at), (parts,), jnp.float32, low / len(cuts), high / len(cuts))
        return jnp.repeat(jnp.exp(draws), extent[axis_at] // parts).reshape((-1,) + (1,) * (len(extent) - axis_at - 1))

    loudness = one(*cuts[0])
    for cut in cuts[1:]:
        loudness = loudness * one(*cut)
    return loudness


def normal_values(key, dims, width, limit, shards=(), kind=jnp.bfloat16):
    level = steps_of(key, dims, shards, -0.22, 0.18) if shards else 1.0
    values = jax.random.normal(key, dims, jnp.float32) * width * level
    return jnp.minimum(jnp.maximum(values, -limit), limit).astype(kind)


def setup_inputs(seed: int = 0) -> dict:
    splits = jax.random.split(jax.random.key(seed), 7)
    return {
        "edge_prec": draw_edge_prec(jax.random.fold_in(splits[6], 71), 0),
        "nugget": jnp.clip(jnp.exp(math.log(0.5) - 2.3025851 * jax.random.uniform(splits[1], (BLOCKS, NODES), jnp.float32) ** steps_of(splits[1], (BLOCKS, NODES), ((0, 2), (1, 64)), -0.2, 0.2)), 0.05, 0.5),
        "arrow": normal_values(splits[2], (FIXED, BLOCKS, NODES), (BLOCKS * NODES) ** -0.5, 0.09375, ((1, 2), (2, 64)), jnp.float32),
        "fixed_prec": draw_fixed_prec(jax.random.fold_in(splits[6], 71), 0),
        "rhs_latent": normal_values(splits[4], (BLOCKS, NODES), 1.0, 6.0, ((0, 2), (1, 64)), jnp.float32),
        "rhs_fixed": normal_values(splits[5], (FIXED,), 1.0, 6.0, (), jnp.float32),
    }


precise = lax.Precision.HIGHEST

def lower_solve(factor, rhs_block):
    return lax.linalg.triangular_solve(factor, rhs_block, left_side=True, lower=True)

def upper_solve(factor, rhs_block):
    return lax.linalg.triangular_solve(factor, rhs_block, left_side=True, lower=True, transpose_a=True)

def reference(edge_prec, nugget, arrow, fixed_prec, rhs_latent, rhs_fixed):
    block_count, node_count = nugget.shape
    fixed_count = arrow.shape[0]
    dtype_used = edge_prec.dtype
    zeros_block = jnp.zeros((1, node_count, node_count), dtype_used)
    following = jnp.concatenate([edge_prec[1:], zeros_block], axis=0)
    identity = jnp.eye(node_count, dtype=dtype_used)
    diagonal = edge_prec + following + nugget[:, :, None] * identity[None]
    after_first = (jnp.arange(block_count) > 0).astype(dtype_used)
    coupling = edge_prec * after_first[:, None, None]
    stacked = jnp.concatenate([arrow, rhs_latent[None]], axis=0)
    stacked = jnp.transpose(stacked, (1, 2, 0))

    def forward(carry, inputs):
        prev_fac, prev_sol = carry
        diag_block, edge_block, rhs_block = inputs
        weight = -lower_solve(prev_fac, edge_block)
        reduced = diag_block - jnp.dot(weight.T, weight, precision=precise)
        factor = jnp.linalg.cholesky(reduced)
        solved = lower_solve(factor, rhs_block - jnp.dot(weight.T, prev_sol, precision=precise))
        return ((factor, solved), (factor, solved, weight))
    initial = (identity, jnp.zeros((node_count, fixed_count + 1), dtype_used))
    _, (factors, forward_sols, weights) = lax.scan(forward, initial, (diagonal, coupling, stacked))
    next_weights = jnp.concatenate([weights[1:], zeros_block], axis=0)

    def backward(after_sol, inputs):
        factor, solved, weight = inputs
        current = upper_solve(factor, solved - jnp.dot(weight, after_sol, precision=precise))
        return (current, current)
    _, values = lax.scan(backward, jnp.zeros((node_count, fixed_count + 1), dtype_used), (factors, forward_sols, next_weights), reverse=True)
    coupled = jnp.einsum('fts,tsj->fj', arrow, values, precision=precise)
    schur_block = fixed_prec - coupled[:, :fixed_count]
    target = rhs_fixed - coupled[:, fixed_count]
    fixed_factor = jnp.linalg.cholesky(schur_block)
    fixed_sol = upper_solve(fixed_factor, lower_solve(fixed_factor, target[:, None]))[:, 0]
    latent = values[:, :, fixed_count] - jnp.einsum('tsf,f->ts', values[:, :, :fixed_count], fixed_sol, precision=precise)
    return (latent, fixed_sol)
```

```python
import functools
import jax, jax.numpy as jnp
from jax import lax
from jax.experimental import pallas as pl
from jax.experimental.pallas import tpu as pltpu

f32=jnp.float32; bf16=jnp.bfloat16
NB=128

def split(x):
    hi=x.astype(bf16); lo=(x-hi.astype(f32)).astype(bf16)
    return hi,lo

def dot3(a,b):
    ah,al=split(a); bh,bl=split(b)
    return jnp.dot(jnp.concatenate([ah,ah,al],axis=1),jnp.concatenate([bh,bl,bh],axis=0),preferred_element_type=f32)

def diag(G):
    n=len(G); lane=lax.broadcasted_iota(jnp.int32,(8,128),1); sub=lax.broadcasted_iota(jnp.int32,(8,128),0)
    G=list(G)
    F=(8,128)
    for j in range(n):
        g=G[j]; o=8*j
        rows=[jnp.broadcast_to(g[s:s+1,:],F) for s in range(8)]
        a=[[jnp.broadcast_to(rows[s][:,o+k:o+k+1],F) for k in range(s+1)] for s in range(8)]
        inb=(lane>=o)&(lane<o+8)
        rows=[jnp.where(inb, jnp.where(lane==o+s,1.0,0.0), rows[s]) for s in range(8)]
        N=[None]*8; r=[None]*8
        for s in range(8):
            r[s]=lax.rsqrt(a[s][s])
            N[s]=rows[s]*r[s]
            l=[None]*8
            for i in range(s+1,8):
                l[i]=a[i][s]*r[s]
            for i in range(s+1,8):
                rows[i]=rows[i]-l[i]*N[s]
                for k in range(s+1,i+1):
                    a[i][k]=a[i][k]-l[i]*l[k]
            for i in range(s+1,8): a[i][s]=l[i]
        out=N[0]
        for s in range(1,8): out=jnp.where(sub==s,N[s],out)
        Z=[None]*8
        for s in reversed(range(8)):
            v=N[s]
            for i in range(s+1,8): v=v-a[i][s]*Z[i]
            Z[s]=v*r[s]
        G[j]=out
        for h in range(j+1,n):
            base=jnp.where(inb,0.0,G[h])
            t=[G[h][:,o+k:o+k+1]*Z[k] for k in range(8)]
            u=((t[0]+t[1])+(t[2]+t[3]))+((t[4]+t[5])+(t[6]+t[7]))
            G[h]=base-u
    return G

def diag_step(D,T,j):
    G=diag([D[8*g:8*g+8,:] for g in range(16)])
    row=lax.broadcasted_iota(jnp.int32,(8,128),0); col=lax.broadcasted_iota(jnp.int32,(8,128),1)
    for g in range(16):
        T[pl.ds(pl.multiple_of(j*NB+8*g,8),8),:]=jnp.where(col<=row+8*g,G[g],0.0)

def small_step(A,D,T,j):
    n=j+1
    o=pl.multiple_of(j*NB,NB); on=pl.multiple_of(n*NB,NB)
    y=dot3(T[pl.ds(o,NB),:],A[pl.ds(o,NB),pl.ds(on,NB)])
    D[...]=A[pl.ds(on,NB),pl.ds(on,NB)]-dot3(y.T,y)

def bulk(A,C,R,M,Rm,T,j,ch=256):
    N=A.shape[0]
    o=pl.multiple_of(j*NB,NB)
    t=T[pl.ds(o,NB),:]
    th,tl=split(t); tk=jnp.concatenate([th,th,tl],axis=1)
    def panel(ref,c0,w):
        x=ref[pl.ds(o,NB),c0:c0+w]
        xh,xl=split(x)
        y=jnp.dot(tk,jnp.concatenate([xh,xl,xh],axis=0),preferred_element_type=f32)
        ref[pl.ds(o,NB),c0:c0+w]=y
        yh,yl=split(y)
        return y,jnp.concatenate([yh,yl,yh],axis=0)
    def trans(y):
        yt=y.T
        h,l=split(yt)
        return jnp.concatenate([h,h,l],axis=1)
    nch=N//ch
    pa=[panel(A,c*ch,ch) for c in range(nch)]
    rowi=lax.broadcasted_iota(jnp.int32,(ch,1),0)
    pr=panel(R,0,128)
    ta=[trans(jnp.where(lax.broadcasted_iota(jnp.int32,(1,ch),1)+c*ch>=o+NB,pa[c][0],0.0)) for c in range(nch)]
    pc=[panel(C,c*ch,ch) for c in range(nch)] if C is not None else []
    tc=[trans(pc[c][0]) for c in range(nch)] if C is not None else []
    def upd(ref,r,c,w,lhs,rhs):
        ref[r*ch:r*ch+ch,c*ch:c*ch+w]-=jnp.dot(lhs,rhs,preferred_element_type=f32)
    for r in range(nch):
        for c in range(r,nch): upd(A,r,c,ch,ta[r],pa[c][1])
        upd(R,r,0,128,ta[r],pr[1])
        for c in range(len(pc)): upd(C,r,c,ch,ta[r],pc[c][1])
    if C is not None:
        for r in range(nch):
            for c in range(r,nch): upd(M,r,c,ch,tc[r],pc[c][1])
            upd(Rm,r,0,128,tc[r],pr[1])

def level(A,C,R,M,Rm,T,D):
    nb=A.shape[0]//NB
    D[...]=A[0:NB,0:NB]
    diag_step(D,T,0)
    small_step(A,D,T,0)
    def body(j,c):
        diag_step(D,T,j)
        bulk(A,C,R,M,Rm,T,j-1)
        @pl.when(j<nb-1)
        def _(): small_step(A,D,T,j)
        return c
    lax.fori_loop(1,nb,body,0)
    bulk(A,C,R,M,Rm,T,nb-1)


def gram(R):
    z=R[...]
    zh,zl=split(z)
    dn=(((0,),(0,)),((),()))
    lhs=jnp.concatenate([zh,zh,zl],axis=0); rhs=jnp.concatenate([zh,zl,zh],axis=0)
    return lax.dot_general(lhs,rhs,dn,preferred_element_type=f32)


def first_kernel(ai,ci,ei,xi,A,C,R,M,X,T,D,sem):
    cps=[pltpu.make_async_copy(s,d,sem.at[i]) for i,(s,d) in enumerate([(ai,A),(ci,C),(ei,M),(xi,R)])]
    for c in cps: c.start()
    for c in cps: c.wait()
    n=A.shape[0]
    lane=lax.broadcasted_iota(jnp.int32,(1,NB),1)
    row=lax.broadcasted_iota(jnp.int32,(NB,n),0); col=lax.broadcasted_iota(jnp.int32,(NB,n),1)
    def init(i,c):
        rows=pl.ds(pl.multiple_of(i*NB,NB),NB)
        x=R[rows,:]
        M[rows,:]=M[rows,:]+C[rows,:]+jnp.where(col==row+i*NB,x[:,64:65],0.0)
        X[rows,:]=jnp.where(lane<17,pltpu.roll(x,96,1),0.0)
        R[rows,:]=jnp.where(lane<17,x,0.0)
        return c
    lax.fori_loop(0,n//NB,init,0)
    level(A,C,R,M,X.at[0:n],T,D)
    X[n:n+NB,:]=gram(R)


def back(A,T,v,x):
    n=A.shape[0]
    for j in reversed(range(n//NB)):
        rows=slice(j*NB,j*NB+NB)
        col=v[rows,0:1]
        if j*NB+NB<n:
            col=col-jnp.sum(A[rows,j*NB+NB:n]*x[:,j*NB+NB:n],axis=1,keepdims=True)
        x[:,rows]=jnp.sum(T[rows,:]*col,axis=0,keepdims=True)


def second_kernel(ai,mi,xi,xm,ci,a1i,c1i,r1i,t1i,fx,O,A,C,R,M,Rm,T,T2,A1,C1,R1,T1,G,D,v,x,sem):
    n=A.shape[0]
    pairs=[(ai,A),(ci,C),(xi.at[0:n],R),(mi,M),(xm.at[0:n],Rm),(a1i,A1),(c1i,C1),(r1i,R1),(t1i,T1),(xi.at[n:n+NB],G.at[0]),(xm.at[n:n+NB],G.at[1])]
    cps=[pltpu.make_async_copy(s,d,sem.at[i]) for i,(s,d) in enumerate(pairs)]
    for c in cps: c.start()
    for c in cps: c.wait()
    level(A,C,R,M,Rm,T,D)
    level(M,None,Rm,None,None,T2,D)
    aug=fx[...]-(G[0]+G[1]+gram(R)+gram(Rm))[0:16,:]
    lane=lax.broadcasted_iota(jnp.int32,(8,NB),1); sub=lax.broadcasted_iota(jnp.int32,(8,NB),0)
    g=diag([aug[0:8,:],aug[8:16,:]])
    f=jnp.zeros((1,NB),f32)
    for i in range(2):
        t=jnp.where(lane<=sub+8*i,g[i],0.0)
        f=f+jnp.sum(t*g[i][:,16:17],axis=0,keepdims=True)
    lane1=lax.broadcasted_iota(jnp.int32,(1,NB),1)
    q=jnp.where(lane1<16,-f,jnp.where(lane1==16,1.0,0.0))
    def rhs(ref):
        return jnp.sum(ref[...]*q,axis=1,keepdims=True)
    v[...]=jnp.broadcast_to(rhs(Rm),v.shape)
    back(M,T2,v,x.at[2:3])
    v[...]=jnp.broadcast_to(rhs(R)-jnp.sum(C[...]*x[2:3,:],axis=1,keepdims=True),v.shape)
    back(A,T,v,x.at[1:2])
    v[...]=jnp.broadcast_to(rhs(R1)-jnp.sum(C1[...]*x[1:2,:],axis=1,keepdims=True),v.shape)
    back(A1,T1,v,x.at[0:1])
    x[3:4,0:NB]=f
    O[...]=x[...]


SHAPE=jax.ShapeDtypeStruct
LIMIT=60*2**20

def first(a,c,e,x):
    n=a.shape[0]
    vm=pltpu.VMEM
    return pl.pallas_call(first_kernel,
        out_shape=[SHAPE((n,n),f32),SHAPE((n,n),f32),SHAPE((n,NB),f32),SHAPE((n,n),f32),SHAPE((n+NB,NB),f32),SHAPE((n,NB),f32)],
        in_specs=[pl.BlockSpec(memory_space=pl.ANY)]*4,out_specs=[pl.BlockSpec(memory_space=vm)]*6,
        scratch_shapes=[vm((NB,NB),f32),pltpu.SemaphoreType.DMA((4,))],
        compiler_params=pltpu.CompilerParams(vmem_limit_bytes=LIMIT),name='first')(a,c,e,x)

def second(a,m,xi,xm,c,a1,c1,r1,t1,fx):
    n=a.shape[0]
    vm=pltpu.VMEM
    big=vm((n,n),f32); tall=vm((n,NB),f32)
    return pl.pallas_call(second_kernel,out_shape=SHAPE((8,n),f32),
        in_specs=[pl.BlockSpec(memory_space=pl.ANY)]*9+[pl.BlockSpec(memory_space=vm)],out_specs=pl.BlockSpec(memory_space=vm),
        scratch_shapes=[big,big,tall,big,tall,tall,tall,big,big,tall,tall,vm((2,NB,NB),f32),vm((NB,NB),f32),tall,vm((8,n),f32),pltpu.SemaphoreType.DMA((11,))],
        compiler_params=pltpu.CompilerParams(vmem_limit_bytes=LIMIT),name='second')(a,m,xi,xm,c,a1,c1,r1,t1,fx)


def body(edge_prec, nugget, arrow, fixed_prec, rhs_latent, rhs_fixed):
    slab=edge_prec.shape[1]
    n=edge_prec.shape[2]
    k=arrow.shape[0]
    tm=lax.axis_index("tm"); blk=lax.axis_index("blk")
    left=tm==0
    swap=[(0,1),(1,0)]
    e0,e1=edge_prec[0],edge_prec[1]
    partner=lax.ppermute(e0,"tm",swap)
    e2=jnp.where(left,partner,e0)
    eye=lax.broadcasted_iota(jnp.int32,(slab,n),1)==lax.broadcasted_iota(jnp.int32,(slab,n),0)+blk*slab
    nug_end=jnp.where(left,nugget[0],nugget[1]); nug_mid=jnp.where(left,nugget[1],nugget[0])
    p=e1+jnp.where(left,e0,0.0)+jnp.where(eye,nug_end[:,None],0.0)
    sign=jnp.where(left,1.0,-1.0)
    r=jnp.concatenate([arrow,rhs_latent[None]],axis=0)
    r_end=jnp.where(left,r[:,0],r[:,1]).T*sign
    r_mid=jnp.where(left,r[:,1],r[:,0]).T*(-sign)
    pad=lambda a,w: jnp.pad(a,((0,0),(0,w-a.shape[1])))
    aux=jnp.concatenate([pad(r_end,32),pad(r_mid,32),pad(nug_mid[:,None],64)],axis=1)
    gather=lambda a: lax.all_gather(a,"blk",axis=0,tiled=True)
    P_=gather(p); C_=gather(e1); E_=gather(e2); X_=gather(aux)
    A1,C1,R1,S,X,T1=first(P_,C_,E_,X_)
    S_o=lax.ppermute(S,"tm",swap); X_o=lax.ppermute(X,"tm",swap)
    fx=jnp.pad(jnp.concatenate([fixed_prec,rhs_fixed[:,None]],axis=1),((0,0),(0,NB-k-1)))
    out=second(S,S_o,X,X_o,E_,A1,C1,R1,T1,fx)
    mine=lax.dynamic_slice(out,(0,blk*slab),(2,slab))
    end=mine[0]*sign; mid=mine[1]*(-sign)
    lat=jnp.stack([jnp.where(left,end,mid),jnp.where(left,mid,end)])
    f=out[3,:k]
    f=jnp.where(left,f,lax.ppermute(f,"tm",[(0,1)]))
    return lat,f


def solution(mesh):
    P=jax.sharding.PartitionSpec
    placed=(P("tm","blk",None),P("tm","blk"),P(None,"tm","blk"),P(),P("tm","blk"),P())
    return jax.shard_map(body,mesh=mesh,in_specs=placed,out_specs=(P("tm","blk"),P()),check_vma=False)
```

```python
import itertools
import jax, jax.numpy as jnp
from jax import lax
from jax.experimental import pallas as pl
from jax.experimental.pallas import tpu as pltpu

f32=jnp.float32; bf16=jnp.bfloat16
NB=128

def split(x):
    hi=x.astype(bf16); lo=(x-hi.astype(f32)).astype(bf16)
    return hi,lo

def dot3(a,b):
    ah,al=split(a); bh,bl=split(b)
    return jnp.dot(jnp.concatenate([ah,ah,al],axis=1),jnp.concatenate([bh,bl,bh],axis=0),preferred_element_type=f32)

def factor(G):
    n=len(G); F=(8,128)
    lane=lax.broadcasted_iota(jnp.int32,F,1); sub=lax.broadcasted_iota(jnp.int32,F,0)
    for j in range(n):
        g=G[j]; o=8*j
        inb=(lane>=o)&(lane<o+8)
        rows=[jnp.broadcast_to(g[s:s+1,:],F) for s in range(8)]
        a=[[jnp.broadcast_to(rows[s][:,o+k:o+k+1],F) for k in range(s+1)] for s in range(8)]
        rows=[jnp.where(inb, jnp.where(lane==o+s,1.0,0.0), rows[s]) for s in range(8)]
        N=[None]*8; r=[None]*8
        if j+1<n:
            cc=[jnp.broadcast_to(G[j+1][:,o+k:o+k+1],F) for k in range(8)]
            nxt=jnp.where(inb,0.0,G[j+1])
        for s in range(8):
            r[s]=lax.rsqrt(a[s][s])
            N[s]=rows[s]*r[s]
            l=[None]*8
            for i in range(s+1,8): l[i]=a[i][s]*r[s]
            for i in range(s+1,8):
                rows[i]=rows[i]-l[i]*N[s]
                for k in range(s+1,i+1): a[i][k]=a[i][k]-l[i]*l[k]
            if j+1<n:
                cs=cc[s]*r[s]
                nxt=nxt-cs*N[s]
                for i in range(s+1,8): cc[i]=cc[i]-l[i]*cs
            for i in range(s+1,8): a[i][s]=l[i]
        out=N[0]
        for s in range(1,8): out=jnp.where(sub==s,N[s],out)
        G[j]=out
        if j+1<n:
            G[j+1]=nxt
        if j+2<n:
            Z=[None]*8
            for s in reversed(range(8)):
                v=N[s]
                for i in reversed(range(s+1,8)): v=v-a[i][s]*Z[i]
                Z[s]=v*r[s]
            for h in range(j+2,n):
                base=jnp.where(inb,0.0,G[h])
                t=[G[h][:,o+k:o+k+1]*Z[k] for k in range(8)]
                u=((t[0]+t[1])+(t[2]+t[3]))+((t[4]+t[5])+(t[6]+t[7]))
                G[h]=base-u
        yield

def diag_step(D,T,j):
    G=[D[8*g:8*g+8,:] for g in range(16)]
    yield from factor(G)
    row=lax.broadcasted_iota(jnp.int32,(8,128),0); col=lax.broadcasted_iota(jnp.int32,(8,128),1)
    for g in range(16):
        T[pl.ds(pl.multiple_of(j*NB+8*g,8),8),:]=jnp.where(col<=row+8*g,G[g],0.0)

def small_step(A,D,T,j):
    n=j+1
    o=pl.multiple_of(j*NB,NB); on=pl.multiple_of(n*NB,NB)
    y=dot3(T[pl.ds(o,NB),:],A[pl.ds(o,NB),pl.ds(on,NB)])
    D[...]=A[pl.ds(on,NB),pl.ds(on,NB)]-dot3(y.T,y)

def bulk(A,C,R,M,Rm,t,j,ch=256):
    N=A.shape[0]
    o=pl.multiple_of(j*NB,NB)
    th,tl=split(t); tk=jnp.concatenate([th,th,tl],axis=1)
    def panel(ref,c0,w):
        x=ref[pl.ds(o,NB),c0:c0+w]
        xh,xl=split(x)
        y=jnp.dot(tk,jnp.concatenate([xh,xl,xh],axis=0),preferred_element_type=f32)
        ref[pl.ds(o,NB),c0:c0+w]=y
        yh,yl=split(y)
        return y,jnp.concatenate([yh,yl,yh],axis=0)
    def trans(y):
        h,l=split(y.T)
        return jnp.concatenate([h,h,l],axis=1)
    def upd(ref,r,c,w,lhs,rhs):
        ref[r*ch:r*ch+ch,c*ch:c*ch+w]-=jnp.dot(lhs,rhs,preferred_element_type=f32)
    nch=N//ch
    lane=lax.broadcasted_iota(jnp.int32,(1,ch),1)
    pa=[None]*nch; pc=[None]*nch; ta=[None]*nch; tc=[None]*nch
    for c in range(nch):
        pa[c]=panel(A,c*ch,ch); yield
    pr=panel(R,0,128); yield
    for c in range(nch):
        ta[c]=trans(jnp.where(lane+c*ch>=o+NB,pa[c][0],0.0)); yield
    if C is not None:
        for c in range(nch):
            pc[c]=panel(C,c*ch,ch); yield
            tc[c]=trans(pc[c][0]); yield
    for r in range(nch):
        for c in range(r,nch):
            upd(A,r,c,ch,ta[r],pa[c][1]); yield
        upd(R,r,0,128,ta[r],pr[1]); yield
        if C is not None:
            for c in range(nch):
                upd(C,r,c,ch,ta[r],pc[c][1]); yield
    if C is not None:
        for r in range(nch):
            for c in range(r,nch):
                upd(M,r,c,ch,tc[r],pc[c][1]); yield
            upd(Rm,r,0,128,tc[r],pr[1]); yield

def drain(g):
    for _ in g: pass

def mix(a,b,na,nb):
    done=0
    for i in range(na):
        while done<(i+1)*nb//na:
            next(b,None); done+=1
        next(a,None)
    drain(b); drain(a)

def level(A,C,R,M,Rm,T,D):
    nb=A.shape[0]//NB
    D[...]=A[0:NB,0:NB]
    drain(diag_step(D,T,0))
    small_step(A,D,T,0)
    pieces=22 if C is None else 60
    def body(j,c):
        t=T[pl.ds(pl.multiple_of((j-1)*NB,NB),NB),:]
        mix(diag_step(D,T,j),bulk(A,C,R,M,Rm,t,j-1),16,pieces)
        @pl.when(j<nb-1)
        def _(): small_step(A,D,T,j)
        return c
    lax.fori_loop(1,nb,body,0)
    drain(bulk(A,C,R,M,Rm,T[(nb-1)*NB:nb*NB,:],nb-1))


def gram(R):
    z=R[...]
    zh,zl=split(z)
    dn=(((0,),(0,)),((),()))
    lhs=jnp.concatenate([zh,zh,zl],axis=0); rhs=jnp.concatenate([zh,zl,zh],axis=0)
    return lax.dot_general(lhs,rhs,dn,preferred_element_type=f32)


SIDE=4


def place():
    blk=lax.axis_index("blk")
    return [blk//(SIDE*SIDE),(blk//SIDE)%SIDE,blk%SIDE]


def beside(at,axis,step):
    at=list(at); at[axis]=lax.rem(at[axis]+step,SIDE)
    return {"blk":(at[0]*SIDE+at[1])*SIDE+at[2]}


def meet(others):
    barrier=pltpu.get_barrier_semaphore()
    for device in others:
        pl.semaphore_signal(barrier,inc=1,device_id=device,device_id_type=pl.DeviceIdType.MESH)
    pl.semaphore_wait(barrier,len(others))


def spread(slab,G,send,recv,local):
    at=place(); rows,lanes=slab.shape; tiles=lanes//NB
    cuts=[0]+[NB*((tiles*(q+1)+2-q)//3) for q in range(3)]; cuts[3]=lanes
    def piece(q,t,coord,part):
        order=[(q+i)%3 for i in range(3)]
        idx=list(at)
        for a in order[:t]: idx[a]=pl.ds(0,SIDE)
        idx[order[t]]=coord
        return G.at[idx[0],idx[1],idx[2],part,cuts[q]:cuts[q+1]]
    whole=pl.ds(0,rows); half=[pl.ds(0,rows//2),pl.ds(rows//2,rows//2)]
    def remote(src,dst,q,t,s,step):
        return pltpu.make_async_remote_copy(src_ref=src,dst_ref=dst,send_sem=send.at[q,t,s],recv_sem=recv.at[q,t,s],
            device_id=beside(at,(q+t)%3,step),device_id_type=pl.DeviceIdType.MESH)
    own=pltpu.make_async_copy(slab,G.at[at[0],at[1],at[2]],local)
    own.start()
    sent=[]
    for t in range(3):
        direct=t<2
        first=[]
        for q in range(3):
            dst=piece(q,t,at[(q+t)%3],whole)
            src=dst if t else slab.at[:,cuts[q]:cuts[q+1]]
            group=[remote(src,dst,q,t,s,step) for s,step in enumerate((1,3,2) if direct else (1,3))]
            for c in group: c.start()
            first.append(group)
        if t==0: own.wait()
        yield
        second=[]
        for q in range(3):
            for c in first[q]: c.wait_recv()
            if not direct:
                for d in range(2):
                    ref=piece(q,t,lax.rem(at[(q+t)%3]+(3 if d==0 else 1),SIDE),half[d])
                    c=remote(ref,ref,q,t,2+d,1 if d==0 else 3); c.start(); second.append(c)
        yield
        for c in second: c.wait_recv()
        sent+=sum(first,[])+second
    for c in sent: c.wait_send()


def neighbours():
    at=place()
    return [beside(at,axis,step) for axis in range(3) for step in (1,2,3)]


def gather_kernel(s1,s2,G1,G2,send,recv,local):
    meet(neighbours())
    gens=[spread(s,G,send.at[i],recv.at[i],local.at[i]) for i,(s,G) in enumerate([(s1,G1),(s2,G2)])]
    for _ in itertools.zip_longest(*gens): pass


def gather(s1,s2):
    shape=lambda s: SHAPE((SIDE,SIDE,SIDE)+s.shape,f32)
    sem=pltpu.SemaphoreType.DMA((2,3,3,4))
    return pl.pallas_call(gather_kernel,out_shape=[shape(s1),shape(s2)],
        in_specs=[pl.BlockSpec(memory_space=pltpu.VMEM)]*2,out_specs=[pl.BlockSpec(memory_space=pl.ANY)]*2,
        scratch_shapes=[sem,sem,pltpu.SemaphoreType.DMA((2,))],
        compiler_params=pltpu.CompilerParams(collective_id=0,has_side_effects=True),name='gather')(s1,s2)


def either(left,a,b,dst,sem):
    @pl.when(left)
    def _(): pltpu.make_async_copy(a,dst,sem).start()
    @pl.when(jnp.logical_not(left))
    def _(): pltpu.make_async_copy(b,dst,sem).start()
    return pltpu.make_async_copy(a,dst,sem)


def copies(pairs,sem):
    out=[pltpu.make_async_copy(s,d,sem.at[i]) for i,(s,d) in enumerate(pairs)]
    for c in out: c.start()
    return out


def tri(n):
    return lax.broadcasted_iota(jnp.int32,(NB,n),0),lax.broadcasted_iota(jnp.int32,(NB,n),1)


def first_kernel(g1,g2,A,C,R,M,X,T,D,sem):
    n=A.shape[0]
    left=lax.axis_index("tm")==0
    cps=copies([(g1.at[:,0:n],A),(g1.at[:,n:n+NB],R)],sem)
    cps.append(either(left,g2,g1.at[:,0:n],C,sem.at[2]))
    for c in cps: c.wait()
    lane=lax.broadcasted_iota(jnp.int32,(1,NB),1)
    row,col=tri(n)
    def init(i,c):
        rows=pl.ds(pl.multiple_of(i*NB,NB),NB)
        x=R[rows,:]
        on=col==row+i*NB
        A[rows,:]=A[rows,:]+jnp.where(on,x[:,64:65],0.0)
        M[rows,:]=C[rows,:]+jnp.where(on,x[:,65:66],0.0)
        X[rows,:]=jnp.where(lane<17,pltpu.roll(x,96,1),0.0)
        R[rows,:]=jnp.where(lane<17,x,0.0)
        return c
    lax.fori_loop(0,n//NB,init,0)
    level(A,C,R,M,X.at[0:n],T,D)
    X[n:n+NB,:]=gram(R)


def second_kernel(d,x,ea,eb,A,C,R,M,X,T,D,sem):
    n=A.shape[0]
    left=lax.axis_index("tm")==0
    cps=copies([(d,A),(x.at[0:n],R)],sem)
    cps.append(either(left,ea,eb,C,sem.at[2]))
    for c in cps: c.wait()
    def init(i,c):
        rows=pl.ds(pl.multiple_of(i*NB,NB),NB)
        e=C[rows,:]
        A[rows,:]=A[rows,:]+e
        M[rows,:]=e
        X[rows,:]=jnp.zeros((NB,NB),f32)
        return c
    lax.fori_loop(0,n//NB,init,0)
    level(A,C,R,M,X.at[0:n],T,D)
    X[n:n+NB,:]=gram(R)


def back(A,T,v,x):
    n=A.shape[0]
    for j in reversed(range(n//NB)):
        rows=slice(j*NB,j*NB+NB)
        col=v[rows,0:1]
        if j*NB+NB<n:
            col=col-jnp.sum(A[rows,j*NB+NB:n]*x[:,j*NB+NB:n],axis=1,keepdims=True)
        x[:,rows]=jnp.sum(T[rows,:]*col,axis=0,keepdims=True)


def fixed(aug):
    lane=lax.broadcasted_iota(jnp.int32,(8,NB),1); sub=lax.broadcasted_iota(jnp.int32,(8,NB),0)
    g=[aug[0:8,:],aug[8:16,:]]
    drain(factor(g))
    f=jnp.zeros((1,NB),f32)
    for i in range(2):
        t=jnp.where(lane<=sub+8*i,g[i],0.0)
        f=f+jnp.sum(t*g[i][:,16:17],axis=0,keepdims=True)
    lane1=lax.broadcasted_iota(jnp.int32,(1,NB),1)
    return f,jnp.where(lane1<16,-f,jnp.where(lane1==16,1.0,0.0))


def third_kernel(m,do,xo,x1,x2,r2,a2,c2,t2,r1,a1,c1,t1,fx,O,A,Q,R,Y,T,A2,C2,T2,R2,A1,C1,T1,R1,X1,X2,D,v,x,sem):
    n=A.shape[0]
    cps=copies([(m,A),(do,Q),(xo,Y),(x2,X2),(x1.at[n:n+NB],X1),(r2,R2),(a2,A2),(c2,C2),(t2,T2),(r1,R1),(a1,A1),(c1,C1),(t1,T1)],sem)
    for c in cps[:5]: c.wait()
    def init(i,c):
        rows=pl.ds(pl.multiple_of(i*NB,NB),NB)
        A[rows,:]=A[rows,:]+Q[rows,:]
        R[rows,:]=Y[rows,:]+X2[rows,:]
        return c
    lax.fori_loop(0,n//NB,init,0)
    level(A,None,R,None,None,T,D)
    f,q=fixed(fx[...]-(X1[...]+Y[n:n+NB,:]+X2[n:n+NB,:]+gram(R))[0:16,:])
    for c in cps[5:]: c.wait()
    def rhs(ref):
        return jnp.sum(ref[...]*q,axis=1,keepdims=True)
    v[...]=jnp.broadcast_to(rhs(R),v.shape)
    back(A,T,v,x.at[2:3])
    v[...]=jnp.broadcast_to(rhs(R2)-jnp.sum(C2[...]*x[2:3,:],axis=1,keepdims=True),v.shape)
    back(A2,T2,v,x.at[1:2])
    v[...]=jnp.broadcast_to(rhs(R1)-jnp.sum(C1[...]*x[1:2,:],axis=1,keepdims=True),v.shape)
    back(A1,T1,v,x.at[0:1])
    x[3:4,0:NB]=f
    O[...]=x[...]


SHAPE=jax.ShapeDtypeStruct
LIMIT=60*2**20


def elimination(kernel,name,n,*args):
    vm=pltpu.VMEM
    return pl.pallas_call(kernel,
        out_shape=[SHAPE((n,n),f32),SHAPE((n,n),f32),SHAPE((n,NB),f32),SHAPE((n,n),f32),SHAPE((n+NB,NB),f32),SHAPE((n,NB),f32)],
        in_specs=[pl.BlockSpec(memory_space=pl.ANY)]*len(args),out_specs=[pl.BlockSpec(memory_space=vm)]*6,
        scratch_shapes=[vm((NB,NB),f32),pltpu.SemaphoreType.DMA((3,))],
        compiler_params=pltpu.CompilerParams(vmem_limit_bytes=LIMIT),name=name)(*args)


def finish(n,*args):
    vm=pltpu.VMEM
    big=vm((n,n),f32); tall=vm((n,NB),f32); plus=vm((n+NB,NB),f32); one=vm((NB,NB),f32)
    return pl.pallas_call(third_kernel,out_shape=SHAPE((8,n),f32),
        in_specs=[pl.BlockSpec(memory_space=pl.ANY)]*13+[pl.BlockSpec(memory_space=vm)],out_specs=pl.BlockSpec(memory_space=vm),
        scratch_shapes=[big,big,tall,plus,tall,big,big,tall,tall,big,big,tall,tall,one,plus,one,tall,vm((8,n),f32),pltpu.SemaphoreType.DMA((13,))],
        compiler_params=pltpu.CompilerParams(vmem_limit_bytes=LIMIT),name='third')(*args)


def body(edge_prec, nugget, arrow, fixed_prec, rhs_latent, rhs_fixed):
    slab=edge_prec.shape[1]; n=edge_prec.shape[2]; k=arrow.shape[0]
    left=lax.axis_index("tm")==0
    swap=[(0,1),(1,0)]
    e0,e1=edge_prec[0],edge_prec[1]
    sign=jnp.where(left,1.0,-1.0)
    ends=lambda a: (jnp.where(left,a[0],a[1]),jnp.where(left,a[1],a[0]))
    nug_end,nug_mid=ends(nugget)
    r_end,r_mid=ends(jnp.moveaxis(jnp.concatenate([arrow,rhs_latent[None]],axis=0),0,-1))
    pad=lambda a,w: jnp.pad(a,((0,0),(0,w-a.shape[1])))
    aux=jnp.concatenate([pad(r_end*sign,32),pad(r_mid*(-sign),32),pad(jnp.stack([nug_end,nug_mid],axis=1),64)],axis=1)
    s1=jnp.concatenate([e1+jnp.where(left,e0,0.0),aux],axis=1)
    s2=jnp.where(left,e1,e0)
    G1,G2=gather(s1,s2)
    G1=G1.reshape(-1,n+NB); G2=G2.reshape(-1,n)
    E=lax.ppermute(G2,"tm",[(1,0)])
    A1,C1,R1,D1,X1,T1=elimination(first_kernel,'first',n,G1,G2)
    D_o=lax.ppermute(D1,"tm",swap); X_o=lax.ppermute(X1,"tm",swap)
    A2,C2,R2,M2,X2,T2=elimination(second_kernel,'second',n,D1,X1,E,G2)
    fx=jnp.pad(jnp.concatenate([fixed_prec,rhs_fixed[:,None]],axis=1),((0,0),(0,NB-k-1)))
    out=finish(n,M2,D_o,X_o,X1,X2,R2,A2,C2,T2,R1,A1,C1,T1,fx)
    mine=lax.dynamic_slice(out,(0,lax.axis_index("blk")*slab),(2,slab))
    end=mine[0]*sign; mid=mine[1]*(-sign)
    lat=jnp.stack([jnp.where(left,end,mid),jnp.where(left,mid,end)])
    f=out[3,:k]
    f=jnp.where(left,f,lax.ppermute(f,"tm",[(0,1)]))
    return lat,f


def solution(mesh):
    P=jax.sharding.PartitionSpec
    placed=(P("tm","blk",None),P("tm","blk"),P(None,"tm","blk"),P(),P("tm","blk"),P())
    return jax.shard_map(body,mesh=mesh,in_specs=placed,out_specs=(P("tm","blk"),P()),check_vma=False)
```

```python
import itertools
import jax, jax.numpy as jnp
from jax import lax
from jax.experimental import pallas as pl
from jax.experimental.pallas import tpu as pltpu

f32=jnp.float32; bf16=jnp.bfloat16
NB=128

def split(x):
    hi=x.astype(bf16); lo=(x-hi.astype(f32)).astype(bf16)
    return hi,lo

def dot3(a,b):
    ah,al=split(a); bh,bl=split(b)
    return jnp.dot(jnp.concatenate([ah,ah,al],axis=1),jnp.concatenate([bh,bl,bh],axis=0),preferred_element_type=f32)

def factor(G):
    n=len(G); F=(8,128)
    lane=lax.broadcasted_iota(jnp.int32,F,1); sub=lax.broadcasted_iota(jnp.int32,F,0)
    down=lambda x,s: jnp.broadcast_to(x[s:s+1,:],F)
    across=lambda x,c: jnp.broadcast_to(x[:,c:c+1],F)
    cols=[across(G[0],k) for k in range(8)]
    for j in range(n):
        g=G[j]; o=8*j
        inb=(lane>=o)&(lane<o+8)
        rows=[jnp.where(inb,jnp.where(lane==o+s,1.0,0.0),down(g,s)) for s in range(8)]
        N=[None]*8; r=[None]*8; L=[None]*8
        more=j+1<n
        if more:
            cc=[across(G[j+1],o+k) for k in range(8)]
            nc=[across(G[j+1],o+8+k) for k in range(8)]
            nxt=jnp.where(inb,0.0,G[j+1])
        for s in range(8):
            d=down(cols[s],s)
            r[s]=lax.rsqrt(d)
            N[s]=rows[s]*r[s]
            low=cols[s]*r[s]
            L[s]=[down(low,i) if i>s else None for i in range(8)]
            inv=1.0/d
            for i in range(s+1,8):
                rows[i]=rows[i]-L[s][i]*N[s]
                cols[i]=cols[i]-(cols[s]*down(cols[s],i))*inv
            if more:
                cs=cc[s]*r[s]
                nxt=nxt-cs*N[s]
                for i in range(s+1,8): cc[i]=cc[i]-L[s][i]*cs
                for k in range(8): nc[k]=nc[k]-cs*down(cs,k)
        out=N[0]
        for s in range(1,8): out=jnp.where(sub==s,N[s],out)
        G[j]=out
        if more:
            G[j+1]=nxt; cols=nc
        if j+2<n:
            Z=[None]*8
            for s in reversed(range(8)):
                v=N[s]
                for i in reversed(range(s+1,8)): v=v-L[s][i]*Z[i]
                Z[s]=v*r[s]
            near=min(n,j+4)
            for h in range(j+2,near):
                t=[across(G[h],o+k)*Z[k] for k in range(8)]
                u=((t[0]+t[1])+(t[2]+t[3]))+((t[4]+t[5])+(t[6]+t[7]))
                G[h]=jnp.where(inb,0.0,G[h])-u
            if near<n:
                z=Z[0]
                for s in range(1,8): z=jnp.where(sub==s,Z[s],z)
                zh=z.astype(bf16).astype(f32)
                def place(x):
                    x=jnp.concatenate([jnp.zeros((o,128),f32)]*(o>0)+[x]+[jnp.zeros((120-o,128),f32)]*(o<120),axis=0)
                    return x.astype(bf16)
                wh,wl=place(zh),place(z-zh)
                first=near//2*2
                lh,ll=split(jnp.concatenate(G[first:],axis=0))
                w=jnp.concatenate([jnp.concatenate([wh,wl],axis=1),jnp.concatenate([wh,jnp.zeros_like(wl)],axis=1)],axis=0)
                u=jnp.dot(jnp.concatenate([lh,ll],axis=1),w,preferred_element_type=f32)
                u=u[:,:128]+u[:,128:]
                for h in range(near,n):
                    G[h]=jnp.where(inb,0.0,G[h])-u[8*(h-first):8*(h-first)+8]
        yield

def diag_step(D,T,j):
    G=[D[8*g:8*g+8,:] for g in range(16)]
    yield from factor(G)
    row=lax.broadcasted_iota(jnp.int32,(8,128),0); col=lax.broadcasted_iota(jnp.int32,(8,128),1)
    for g in range(16):
        T[pl.ds(pl.multiple_of(j*NB+8*g,8),8),:]=jnp.where(col<=row+8*g,G[g],0.0)

def small_step(A,D,T,j):
    n=j+1
    o=pl.multiple_of(j*NB,NB); on=pl.multiple_of(n*NB,NB)
    y=dot3(T[pl.ds(o,NB),:],A[pl.ds(o,NB),pl.ds(on,NB)])
    D[...]=A[pl.ds(on,NB),pl.ds(on,NB)]-dot3(y.T,y)

def bulk(A,C,R,M,Rm,t,j,low=0,ch=256):
    N=A.shape[0]
    o=pl.multiple_of(j*NB,NB)
    th,tl=split(t); tk=jnp.concatenate([th,th,tl],axis=1)
    def panel(ref,c0,w):
        x=ref[pl.ds(o,NB),c0:c0+w]
        xh,xl=split(x)
        y=jnp.dot(tk,jnp.concatenate([xh,xl,xh],axis=0),preferred_element_type=f32)
        ref[pl.ds(o,NB),c0:c0+w]=y
        yh,yl=split(y)
        return y,jnp.concatenate([yh,yl,yh],axis=0)
    def trans(y):
        h,l=split(y.T)
        return jnp.concatenate([h,h,l],axis=1)
    def upd(ref,r,c,w,lhs,rhs):
        ref[r*ch:r*ch+ch,c*ch:c*ch+w]-=jnp.dot(lhs,rhs,preferred_element_type=f32)
    nch=N//ch
    lane=lax.broadcasted_iota(jnp.int32,(1,ch),1)
    pa=[None]*nch; pc=[None]*nch; ta=[None]*nch; tc=[None]*nch
    for c in range(low,nch):
        pa[c]=panel(A,c*ch,ch); yield
    pr=panel(R,0,128); yield
    for c in range(low,nch):
        ta[c]=trans(jnp.where(lane+c*ch>=o+NB,pa[c][0],0.0)); yield
    if C is not None:
        for c in range(nch):
            pc[c]=panel(C,c*ch,ch); yield
            tc[c]=trans(pc[c][0]); yield
    for r in range(low,nch):
        for c in range(r,nch):
            upd(A,r,c,ch,ta[r],pa[c][1]); yield
        upd(R,r,0,128,ta[r],pr[1]); yield
        if C is not None:
            for c in range(nch):
                upd(C,r,c,ch,ta[r],pc[c][1]); yield
    if C is not None:
        for r in range(nch):
            for c in range(r,nch):
                upd(M,r,c,ch,tc[r],pc[c][1]); yield
            upd(Rm,r,0,128,tc[r],pr[1]); yield

def drain(g):
    for _ in g: pass

def mix(a,b,na,nb):
    done=0
    for i in range(na):
        while done<(i+1)*nb//na:
            next(b,None); done+=1
        next(a,None)
    drain(b); drain(a)

def pieces(nch,low,coupled):
    left=nch-low
    count=2*left+1+left*(left+1)//2+left
    return count+(2*nch+left*nch+nch*(nch+1)//2+nch if coupled else 0)

def level(A,C,R,M,Rm,T,D,ready=None,done=None,ch=256):
    nb=A.shape[0]//NB; nch=A.shape[0]//ch; per=ch//NB
    D[...]=A[0:NB,0:NB]
    drain(diag_step(D,T,0))
    small_step(A,D,T,0)
    if ready is not None: ready()
    def make(low):
        def body(j,c):
            t=T[pl.ds(pl.multiple_of((j-1)*NB,NB),NB),:]
            mix(diag_step(D,T,j),bulk(A,C,R,M,Rm,t,j-1,low),16,pieces(nch,low,C is not None))
            @pl.when(j<nb-1)
            def _(): small_step(A,D,T,j)
            return c
        return body
    if C is None:
        lax.fori_loop(1,nb,make(0),0)
    else:
        for low in range(nch):
            lax.fori_loop(max(1,low*per),low*per+per,make(low),0)
            done(low)
    drain(bulk(A,C,R,M,Rm,T[(nb-1)*NB:nb*NB,:],nb-1,nch))


def gram(R):
    z=R[...]
    zh,zl=split(z)
    dn=(((0,),(0,)),((),()))
    lhs=jnp.concatenate([zh,zh,zl],axis=0); rhs=jnp.concatenate([zh,zl,zh],axis=0)
    return lax.dot_general(lhs,rhs,dn,preferred_element_type=f32)


SIDE=4


def place():
    blk=lax.axis_index("blk")
    return [blk//(SIDE*SIDE),(blk//SIDE)%SIDE,blk%SIDE]


def beside(at,axis,step):
    at=list(at); at[axis]=lax.rem(at[axis]+step,SIDE)
    return {"blk":(at[0]*SIDE+at[1])*SIDE+at[2]}


def meet(others):
    barrier=pltpu.get_barrier_semaphore()
    for device in others:
        pl.semaphore_signal(barrier,inc=1,device_id=device,device_id_type=pl.DeviceIdType.MESH)
    pl.semaphore_wait(barrier,len(others))


def spread(slab,G,send,recv,local):
    at=place(); rows,lanes=slab.shape; tiles=lanes//NB
    cuts=[0]+[NB*((tiles*(q+1)+2-q)//3) for q in range(3)]; cuts[3]=lanes
    def piece(q,t,coord,part):
        order=[(q+i)%3 for i in range(3)]
        idx=list(at)
        for a in order[:t]: idx[a]=pl.ds(0,SIDE)
        idx[order[t]]=coord
        return G.at[idx[0],idx[1],idx[2],part,cuts[q]:cuts[q+1]]
    whole=pl.ds(0,rows); half=[pl.ds(0,rows//2),pl.ds(rows//2,rows//2)]
    def remote(src,dst,q,t,s,step):
        return pltpu.make_async_remote_copy(src_ref=src,dst_ref=dst,send_sem=send.at[q,t,s],recv_sem=recv.at[q,t,s],
            device_id=beside(at,(q+t)%3,step),device_id_type=pl.DeviceIdType.MESH)
    own=pltpu.make_async_copy(slab,G.at[at[0],at[1],at[2]],local)
    own.start()
    sent=[]
    for t in range(3):
        direct=t<2
        first=[]
        for q in range(3):
            dst=piece(q,t,at[(q+t)%3],whole)
            src=dst if t else slab.at[:,cuts[q]:cuts[q+1]]
            group=[remote(src,dst,q,t,s,step) for s,step in enumerate((1,3,2) if direct else (1,3))]
            for c in group: c.start()
            first.append(group)
        if t==0: own.wait()
        yield
        second=[]
        for q in range(3):
            for c in first[q]: c.wait_recv()
            if not direct:
                for d in range(2):
                    ref=piece(q,t,lax.rem(at[(q+t)%3]+(3 if d==0 else 1),SIDE),half[d])
                    c=remote(ref,ref,q,t,2+d,1 if d==0 else 3); c.start(); second.append(c)
        yield
        for c in second: c.wait_recv()
        sent+=sum(first,[])+second
    for c in sent: c.wait_send()


def neighbours():
    at=place()
    return [beside(at,axis,step) for axis in range(3) for step in (1,2,3)]


def gather_kernel(s1,s2,G1,G2,send,recv,local):
    meet(neighbours())
    gens=[spread(s,G,send.at[i],recv.at[i],local.at[i]) for i,(s,G) in enumerate([(s1,G1),(s2,G2)])]
    for _ in itertools.zip_longest(*gens): pass


def gather(s1,s2):
    shape=lambda s: SHAPE((SIDE,SIDE,SIDE)+s.shape,f32)
    sem=pltpu.SemaphoreType.DMA((2,3,3,4))
    return pl.pallas_call(gather_kernel,out_shape=[shape(s1),shape(s2)],
        in_specs=[pl.BlockSpec(memory_space=pltpu.VMEM)]*2,out_specs=[pl.BlockSpec(memory_space=pl.ANY)]*2,
        scratch_shapes=[sem,sem,pltpu.SemaphoreType.DMA((2,))],
        compiler_params=pltpu.CompilerParams(collective_id=0,has_side_effects=True),name='gather')(s1,s2)


def either(left,a,b,dst,sem):
    @pl.when(left)
    def _(): pltpu.make_async_copy(a,dst,sem).start()
    @pl.when(jnp.logical_not(left))
    def _(): pltpu.make_async_copy(b,dst,sem).start()
    return pltpu.make_async_copy(a,dst,sem)


def copies(pairs,sem):
    out=[pltpu.make_async_copy(s,d,sem.at[i]) for i,(s,d) in enumerate(pairs)]
    for c in out: c.start()
    return out


def tri(n):
    return lax.broadcasted_iota(jnp.int32,(NB,n),0),lax.broadcasted_iota(jnp.int32,(NB,n),1)


def leaving(A,C,Ao,Co,sem):
    n=A.shape[0]; per=2
    started=[]
    def go(src,dst,lo,hi):
        c=pltpu.make_async_copy(src.at[lo:hi],dst.at[lo:hi],sem.at[len(started)])
        c.start(); started.append(c)
    def done(low):
        lo,hi=max(0,(per*low-1)*NB),(per*low+1)*NB
        last=hi+NB==n
        go(A,Ao,lo,n if last else hi)
        go(C,Co,lo,hi)
    def end():
        go(C,Co,n-NB,n)
        for c in started: c.wait()
    return done,end


def first_kernel(g1,g2,Ao,Co,R,M,X,T,A,C,D,sem,osem):
    n=A.shape[0]
    left=lax.axis_index("tm")==0
    cps=copies([(g1.at[:,0:n],A),(g1.at[:,n:n+NB],R)],sem)
    late=either(left,g2,g1.at[:,0:n],C,sem.at[2])
    for c in cps: c.wait()
    lane=lax.broadcasted_iota(jnp.int32,(1,NB),1)
    row,col=tri(n)
    def early(i,c):
        rows=pl.ds(pl.multiple_of(i*NB,NB),NB)
        A[rows,:]=A[rows,:]+jnp.where(col==row+i*NB,R[rows,64:65],0.0)
        return c
    lax.fori_loop(0,n//NB,early,0)
    def ready():
        late.wait()
        def init(i,c):
            rows=pl.ds(pl.multiple_of(i*NB,NB),NB)
            x=R[rows,:]
            M[rows,:]=C[rows,:]+jnp.where(col==row+i*NB,x[:,65:66],0.0)
            X[rows,:]=jnp.where(lane<17,pltpu.roll(x,96,1),0.0)
            R[rows,:]=jnp.where(lane<17,x,0.0)
            return c
        lax.fori_loop(0,n//NB,init,0)
    done,end=leaving(A,C,Ao,Co,osem)
    level(A,C,R,M,X.at[0:n],T,D,ready,done)
    X[n:n+NB,:]=gram(R)
    end()


def second_kernel(d,x,ea,eb,Ao,Co,R,M,X,T,A,C,D,sem,osem):
    n=A.shape[0]
    left=lax.axis_index("tm")==0
    cps=copies([(d,A),(x.at[0:n],R)],sem)
    cps.append(either(left,ea,eb,C,sem.at[2]))
    for c in cps: c.wait()
    def early(i,c):
        rows=pl.ds(pl.multiple_of(i*NB,NB),NB)
        A[rows,:]=A[rows,:]+C[rows,:]
        return c
    lax.fori_loop(0,n//NB,early,0)
    def ready():
        def init(i,c):
            rows=pl.ds(pl.multiple_of(i*NB,NB),NB)
            M[rows,:]=C[rows,:]
            X[rows,:]=jnp.zeros((NB,NB),f32)
            return c
        lax.fori_loop(0,n//NB,init,0)
    done,end=leaving(A,C,Ao,Co,osem)
    level(A,C,R,M,X.at[0:n],T,D,ready,done)
    X[n:n+NB,:]=gram(R)
    end()


def back(A,T,v,x):
    n=A.shape[0]
    for j in reversed(range(n//NB)):
        rows=slice(j*NB,j*NB+NB)
        col=v[rows,0:1]
        if j*NB+NB<n:
            col=col-jnp.sum(A[rows,j*NB+NB:n]*x[:,j*NB+NB:n],axis=1,keepdims=True)
        x[:,rows]=jnp.sum(T[rows,:]*col,axis=0,keepdims=True)


def fixed(aug):
    lane=lax.broadcasted_iota(jnp.int32,(8,NB),1); sub=lax.broadcasted_iota(jnp.int32,(8,NB),0)
    g=[aug[0:8,:],aug[8:16,:]]
    drain(factor(g))
    f=jnp.zeros((1,NB),f32)
    for i in range(2):
        t=jnp.where(lane<=sub+8*i,g[i],0.0)
        f=f+jnp.sum(t*g[i][:,16:17],axis=0,keepdims=True)
    lane1=lax.broadcasted_iota(jnp.int32,(1,NB),1)
    return f,jnp.where(lane1<16,-f,jnp.where(lane1==16,1.0,0.0))


def third_kernel(m,do,xo,x1,x2,r2,a2,c2,t2,r1,a1,c1,t1,fx,O,A,Q,R,Y,T,A2,C2,T2,R2,A1,C1,T1,R1,X1,X2,D,v,x,sem):
    n=A.shape[0]
    cps=copies([(m,A),(do,Q),(xo,Y),(x2,X2),(x1.at[n:n+NB],X1),(r2,R2),(a2,A2),(c2,C2),(t2,T2),(r1,R1),(a1,A1),(c1,C1),(t1,T1)],sem)
    for c in cps[:5]: c.wait()
    def init(i,c):
        rows=pl.ds(pl.multiple_of(i*NB,NB),NB)
        A[rows,:]=A[rows,:]+Q[rows,:]
        R[rows,:]=Y[rows,:]+X2[rows,:]
        return c
    lax.fori_loop(0,n//NB,init,0)
    level(A,None,R,None,None,T,D)
    f,q=fixed(fx[...]-(X1[...]+Y[n:n+NB,:]+X2[n:n+NB,:]+gram(R))[0:16,:])
    for c in cps[5:]: c.wait()
    def rhs(ref):
        return jnp.sum(ref[...]*q,axis=1,keepdims=True)
    v[...]=jnp.broadcast_to(rhs(R),v.shape)
    back(A,T,v,x.at[2:3])
    v[...]=jnp.broadcast_to(rhs(R2)-jnp.sum(C2[...]*x[2:3,:],axis=1,keepdims=True),v.shape)
    back(A2,T2,v,x.at[1:2])
    v[...]=jnp.broadcast_to(rhs(R1)-jnp.sum(C1[...]*x[1:2,:],axis=1,keepdims=True),v.shape)
    back(A1,T1,v,x.at[0:1])
    x[3:4,0:NB]=f
    O[...]=x[...]


SHAPE=jax.ShapeDtypeStruct
LIMIT=60*2**20


def elimination(kernel,name,n,*args):
    vm=pltpu.VMEM
    return pl.pallas_call(kernel,
        out_shape=[SHAPE((n,n),f32),SHAPE((n,n),f32),SHAPE((n,NB),f32),SHAPE((n,n),f32),SHAPE((n+NB,NB),f32),SHAPE((n,NB),f32)],
        in_specs=[pl.BlockSpec(memory_space=pl.ANY)]*len(args),
        out_specs=[pl.BlockSpec(memory_space=pl.ANY)]*2+[pl.BlockSpec(memory_space=vm)]*4,
        scratch_shapes=[vm((n,n),f32),vm((n,n),f32),vm((NB,NB),f32),pltpu.SemaphoreType.DMA((3,)),pltpu.SemaphoreType.DMA((9,))],
        compiler_params=pltpu.CompilerParams(vmem_limit_bytes=LIMIT),name=name)(*args)


def finish(n,*args):
    vm=pltpu.VMEM
    big=vm((n,n),f32); tall=vm((n,NB),f32); plus=vm((n+NB,NB),f32); one=vm((NB,NB),f32)
    return pl.pallas_call(third_kernel,out_shape=SHAPE((8,n),f32),
        in_specs=[pl.BlockSpec(memory_space=pl.ANY)]*13+[pl.BlockSpec(memory_space=vm)],out_specs=pl.BlockSpec(memory_space=vm),
        scratch_shapes=[big,big,tall,plus,tall,big,big,tall,tall,big,big,tall,tall,one,plus,one,tall,vm((8,n),f32),pltpu.SemaphoreType.DMA((13,))],
        compiler_params=pltpu.CompilerParams(vmem_limit_bytes=LIMIT),name='third')(*args)


def body(edge_prec, nugget, arrow, fixed_prec, rhs_latent, rhs_fixed):
    slab=edge_prec.shape[1]; n=edge_prec.shape[2]; k=arrow.shape[0]
    left=lax.axis_index("tm")==0
    swap=[(0,1),(1,0)]
    e0,e1=edge_prec[0],edge_prec[1]
    sign=jnp.where(left,1.0,-1.0)
    ends=lambda a: (jnp.where(left,a[0],a[1]),jnp.where(left,a[1],a[0]))
    nug_end,nug_mid=ends(nugget)
    r_end,r_mid=ends(jnp.moveaxis(jnp.concatenate([arrow,rhs_latent[None]],axis=0),0,-1))
    pad=lambda a,w: jnp.pad(a,((0,0),(0,w-a.shape[1])))
    aux=jnp.concatenate([pad(r_end*sign,32),pad(r_mid*(-sign),32),pad(jnp.stack([nug_end,nug_mid],axis=1),64)],axis=1)
    s1=jnp.concatenate([e1+jnp.where(left,e0,0.0),aux],axis=1)
    s2=jnp.where(left,e1,e0)
    G1,G2=gather(s1,s2)
    G1=G1.reshape(-1,n+NB); G2=G2.reshape(-1,n)
    E=lax.ppermute(G2,"tm",[(1,0)])
    A1,C1,R1,D1,X1,T1=elimination(first_kernel,'first',n,G1,G2)
    D_o=lax.ppermute(D1,"tm",swap); X_o=lax.ppermute(X1,"tm",swap)
    A2,C2,R2,M2,X2,T2=elimination(second_kernel,'second',n,D1,X1,E,G2)
    fx=jnp.pad(jnp.concatenate([fixed_prec,rhs_fixed[:,None]],axis=1),((0,0),(0,NB-k-1)))
    out=finish(n,M2,D_o,X_o,X1,X2,R2,A2,C2,T2,R1,A1,C1,T1,fx)
    mine=lax.dynamic_slice(out,(0,lax.axis_index("blk")*slab),(2,slab))
    end=mine[0]*sign; mid=mine[1]*(-sign)
    lat=jnp.stack([jnp.where(left,end,mid),jnp.where(left,mid,end)])
    f=out[3,:k]
    f=jnp.where(left,f,lax.ppermute(f,"tm",[(0,1)]))
    return lat,f


def solution(mesh):
    P=jax.sharding.PartitionSpec
    placed=(P("tm","blk",None),P("tm","blk"),P(None,"tm","blk"),P(),P("tm","blk"),P())
    return jax.shard_map(body,mesh=mesh,in_specs=placed,out_specs=(P("tm","blk"),P()),check_vma=False)
```

```python
import itertools
import jax, jax.numpy as jnp
from jax import lax
from jax.experimental import pallas as pl
from jax.experimental.pallas import tpu as pltpu

f32=jnp.float32; bf16=jnp.bfloat16
NB=128

def split(x):
    hi=x.astype(bf16); lo=(x-hi.astype(f32)).astype(bf16)
    return hi,lo

def dot3(a,b):
    ah,al=split(a); bh,bl=split(b)
    return jnp.dot(jnp.concatenate([ah,ah,al],axis=1),jnp.concatenate([bh,bl,bh],axis=0),preferred_element_type=f32)

def factor(G):
    n=len(G); F=(8,128)
    lane=lax.broadcasted_iota(jnp.int32,F,1); sub=lax.broadcasted_iota(jnp.int32,F,0)
    down=lambda x,s: jnp.broadcast_to(x[s:s+1,:],F)
    across=lambda x,c: jnp.broadcast_to(x[:,c:c+1],F)
    cols=[across(G[0],k) for k in range(8)]
    for j in range(n):
        g=G[j]; o=8*j
        inb=(lane>=o)&(lane<o+8)
        rows=[jnp.where(inb,jnp.where(lane==o+s,1.0,0.0),down(g,s)) for s in range(8)]
        N=[None]*8; r=[None]*8; L=[None]*8
        more=j+1<n
        if more:
            cc=[across(G[j+1],o+k) for k in range(8)]
            nc=[across(G[j+1],o+8+k) for k in range(8)]
            nxt=jnp.where(inb,0.0,G[j+1])
        for s in range(8):
            d=down(cols[s],s)
            r[s]=lax.rsqrt(d)
            N[s]=rows[s]*r[s]
            low=cols[s]*r[s]
            L[s]=[down(low,i) if i>s else None for i in range(8)]
            inv=1.0/d
            for i in range(s+1,8):
                rows[i]=rows[i]-L[s][i]*N[s]
                cols[i]=cols[i]-(cols[s]*down(cols[s],i))*inv
            if more:
                cs=cc[s]*r[s]
                nxt=nxt-cs*N[s]
                for i in range(s+1,8): cc[i]=cc[i]-L[s][i]*cs
                for k in range(8): nc[k]=nc[k]-cs*down(cs,k)
        out=N[0]
        for s in range(1,8): out=jnp.where(sub==s,N[s],out)
        G[j]=out
        if more:
            G[j+1]=nxt; cols=nc
        if j+2<n:
            Z=[None]*8
            for s in reversed(range(8)):
                v=N[s]
                for i in reversed(range(s+1,8)): v=v-L[s][i]*Z[i]
                Z[s]=v*r[s]
            near=min(n,j+4)
            for h in range(j+2,near):
                t=[across(G[h],o+k)*Z[k] for k in range(8)]
                u=((t[0]+t[1])+(t[2]+t[3]))+((t[4]+t[5])+(t[6]+t[7]))
                G[h]=jnp.where(inb,0.0,G[h])-u
            if near<n:
                z=Z[0]
                for s in range(1,8): z=jnp.where(sub==s,Z[s],z)
                zh=z.astype(bf16).astype(f32)
                def place(x):
                    x=jnp.concatenate([jnp.zeros((o,128),f32)]*(o>0)+[x]+[jnp.zeros((120-o,128),f32)]*(o<120),axis=0)
                    return x.astype(bf16)
                wh,wl=place(zh),place(z-zh)
                first=near//2*2
                lh,ll=split(jnp.concatenate(G[first:],axis=0))
                w=jnp.concatenate([jnp.concatenate([wh,wl],axis=1),jnp.concatenate([wh,jnp.zeros_like(wl)],axis=1)],axis=0)
                u=jnp.dot(jnp.concatenate([lh,ll],axis=1),w,preferred_element_type=f32)
                u=u[:,:128]+u[:,128:]
                for h in range(near,n):
                    G[h]=jnp.where(inb,0.0,G[h])-u[8*(h-first):8*(h-first)+8]
        yield

def diag_step(D,T,j):
    G=[D[8*g:8*g+8,:] for g in range(16)]
    yield from factor(G)
    row=lax.broadcasted_iota(jnp.int32,(8,128),0); col=lax.broadcasted_iota(jnp.int32,(8,128),1)
    for g in range(16):
        T[pl.ds(pl.multiple_of(j*NB+8*g,8),8),:]=jnp.where(col<=row+8*g,G[g],0.0)

def small_step(A,D,T,j):
    n=j+1
    o=pl.multiple_of(j*NB,NB); on=pl.multiple_of(n*NB,NB)
    y=dot3(T[pl.ds(o,NB),:],A[pl.ds(o,NB),pl.ds(on,NB)])
    D[...]=A[pl.ds(on,NB),pl.ds(on,NB)]-dot3(y.T,y)

def bulk(A,C,R,M,Rm,t,j,low=0,ch=256):
    N=A.shape[0]
    o=pl.multiple_of(j*NB,NB)
    th,tl=split(t); tk=jnp.concatenate([th,th,tl],axis=1)
    def panel(ref,c0,w):
        x=ref[pl.ds(o,NB),c0:c0+w]
        xh,xl=split(x)
        y=jnp.dot(tk,jnp.concatenate([xh,xl,xh],axis=0),preferred_element_type=f32)
        ref[pl.ds(o,NB),c0:c0+w]=y
        yh,yl=split(y)
        return y,jnp.concatenate([yh,yl,yh],axis=0)
    def trans(y):
        h,l=split(y.T)
        return jnp.concatenate([h,h,l],axis=1)
    def upd(ref,r,c,w,lhs,rhs):
        ref[r*ch:r*ch+ch,c*ch:c*ch+w]-=jnp.dot(lhs,rhs,preferred_element_type=f32)
    nch=N//ch
    lane=lax.broadcasted_iota(jnp.int32,(1,ch),1)
    pa=[None]*nch; pc=[None]*nch; ta=[None]*nch; tc=[None]*nch
    for c in range(low,nch):
        pa[c]=panel(A,c*ch,ch); yield
    pr=panel(R,0,128); yield
    for c in range(low,nch):
        ta[c]=trans(jnp.where(lane+c*ch>=o+NB,pa[c][0],0.0)); yield
    if C is not None:
        for c in range(nch):
            pc[c]=panel(C,c*ch,ch); yield
            tc[c]=trans(pc[c][0]); yield
    for r in range(low,nch):
        for c in range(r,nch):
            upd(A,r,c,ch,ta[r],pa[c][1]); yield
        upd(R,r,0,128,ta[r],pr[1]); yield
        if C is not None:
            for c in range(nch):
                upd(C,r,c,ch,ta[r],pc[c][1]); yield
    if C is not None:
        for r in range(nch):
            for c in range(r,nch):
                upd(M,r,c,ch,tc[r],pc[c][1]); yield
            upd(Rm,r,0,128,tc[r],pr[1]); yield

def drain(g):
    for _ in g: pass

def mix(a,b,na,nb):
    done=0
    for i in range(na):
        while done<(i+1)*nb//na:
            next(b,None); done+=1
        next(a,None)
    drain(b); drain(a)

def pieces(nch,low,coupled):
    left=nch-low
    count=2*left+1+left*(left+1)//2+left
    return count+(2*nch+left*nch+nch*(nch+1)//2+nch if coupled else 0)

def level(A,C,R,M,Rm,T,D,ready=None,done=None,ch=256):
    nb=A.shape[0]//NB; nch=A.shape[0]//ch; per=ch//NB
    D[...]=A[0:NB,0:NB]
    drain(diag_step(D,T,0))
    small_step(A,D,T,0)
    if ready is not None: ready()
    def make(low):
        def body(j,c):
            t=T[pl.ds(pl.multiple_of((j-1)*NB,NB),NB),:]
            mix(diag_step(D,T,j),bulk(A,C,R,M,Rm,t,j-1,low),16,pieces(nch,low,C is not None))
            @pl.when(j<nb-1)
            def _(): small_step(A,D,T,j)
            return c
        return body
    if C is None:
        lax.fori_loop(1,nb,make(0),0)
    else:
        for low in range(nch):
            lax.fori_loop(max(1,low*per),low*per+per,make(low),0)
            done(low)
    drain(bulk(A,C,R,M,Rm,T[(nb-1)*NB:nb*NB,:],nb-1,nch))


def gram(R):
    z=R[...]
    zh,zl=split(z)
    dn=(((0,),(0,)),((),()))
    lhs=jnp.concatenate([zh,zh,zl],axis=0); rhs=jnp.concatenate([zh,zl,zh],axis=0)
    return lax.dot_general(lhs,rhs,dn,preferred_element_type=f32)


SIDE=4


def place():
    blk=lax.axis_index("blk")
    return [blk//(SIDE*SIDE),(blk//SIDE)%SIDE,blk%SIDE]


def beside(at,axis,step):
    at=list(at); at[axis]=lax.rem(at[axis]+step,SIDE)
    return {"blk":(at[0]*SIDE+at[1])*SIDE+at[2]}


def meet(others):
    barrier=pltpu.get_barrier_semaphore()
    for device in others:
        pl.semaphore_signal(barrier,inc=1,device_id=device,device_id_type=pl.DeviceIdType.MESH)
    pl.semaphore_wait(barrier,len(others))


def spread(slab,G,send,recv,local):
    at=place(); rows,lanes=slab.shape; tiles=lanes//NB
    cuts=[0]+[NB*((tiles*(q+1)+2-q)//3) for q in range(3)]; cuts[3]=lanes
    def piece(q,t,coord,part):
        order=[(q+i)%3 for i in range(3)]
        idx=list(at)
        for a in order[:t]: idx[a]=pl.ds(0,SIDE)
        idx[order[t]]=coord
        return G.at[idx[0],idx[1],idx[2],part,cuts[q]:cuts[q+1]]
    whole=pl.ds(0,rows); half=[pl.ds(0,rows//2),pl.ds(rows//2,rows//2)]
    def remote(src,dst,q,t,s,step):
        return pltpu.make_async_remote_copy(src_ref=src,dst_ref=dst,send_sem=send.at[q,t,s],recv_sem=recv.at[q,t,s],
            device_id=beside(at,(q+t)%3,step),device_id_type=pl.DeviceIdType.MESH)
    own=pltpu.make_async_copy(slab,G.at[at[0],at[1],at[2]],local)
    own.start()
    sent=[]
    for t in range(3):
        direct=t<2
        first=[]
        for q in range(3):
            dst=piece(q,t,at[(q+t)%3],whole)
            src=dst if t else slab.at[:,cuts[q]:cuts[q+1]]
            group=[remote(src,dst,q,t,s,step) for s,step in enumerate((1,3,2) if direct else (1,3))]
            for c in group: c.start()
            first.append(group)
        if t==0: own.wait()
        yield
        second=[]
        for q in range(3):
            for c in first[q]: c.wait_recv()
            if not direct:
                for d in range(2):
                    ref=piece(q,t,lax.rem(at[(q+t)%3]+(3 if d==0 else 1),SIDE),half[d])
                    c=remote(ref,ref,q,t,2+d,1 if d==0 else 3); c.start(); second.append(c)
        yield
        for c in second: c.wait_recv()
        sent+=sum(first,[])+second
    for c in sent: c.wait_send()


def neighbours():
    at=place()
    return [beside(at,axis,step) for axis in range(3) for step in (1,2,3)]


def gather_kernel(edge,aux,G1,G2,s1,s2,send,recv,local):
    n=edge.shape[2]
    left=lax.axis_index("tm")==0
    e0,e1=edge[0],edge[1]
    s1[:,0:n]=e1+jnp.where(left,e0,0.0)
    s1[:,n:n+NB]=aux[...]
    s2[...]=jnp.where(left,e1,e0)
    meet(neighbours())
    gens=[spread(s,G,send.at[i],recv.at[i],local.at[i]) for i,(s,G) in enumerate([(s1,G1),(s2,G2)])]
    for _ in itertools.zip_longest(*gens): pass


def gather(edge,aux):
    rows,n=edge.shape[1:]
    shape=lambda w: SHAPE((SIDE,SIDE,SIDE,rows,w),f32)
    sem=pltpu.SemaphoreType.DMA((2,3,3,4))
    vm=pltpu.VMEM
    return pl.pallas_call(gather_kernel,out_shape=[shape(n+NB),shape(n)],
        in_specs=[pl.BlockSpec(memory_space=vm)]*2,out_specs=[pl.BlockSpec(memory_space=pl.ANY)]*2,
        scratch_shapes=[vm((rows,n+NB),f32),vm((rows,n),f32),sem,sem,pltpu.SemaphoreType.DMA((2,))],
        compiler_params=pltpu.CompilerParams(collective_id=0,has_side_effects=True),name='gather')(edge,aux)


def either(left,a,b,dst,sem):
    @pl.when(left)
    def _(): pltpu.make_async_copy(a,dst,sem).start()
    @pl.when(jnp.logical_not(left))
    def _(): pltpu.make_async_copy(b,dst,sem).start()
    return pltpu.make_async_copy(a,dst,sem)


def copies(pairs,sem):
    out=[pltpu.make_async_copy(s,d,sem.at[i]) for i,(s,d) in enumerate(pairs)]
    for c in out: c.start()
    return out


def tri(n):
    return lax.broadcasted_iota(jnp.int32,(NB,n),0),lax.broadcasted_iota(jnp.int32,(NB,n),1)


def leaving(A,C,Ao,Co,sem):
    n=A.shape[0]; per=2
    started=[]
    def go(src,dst,lo,hi):
        c=pltpu.make_async_copy(src.at[lo:hi],dst.at[lo:hi],sem.at[len(started)])
        c.start(); started.append(c)
    def done(low):
        lo,hi=max(0,(per*low-1)*NB),(per*low+1)*NB
        last=hi+NB==n
        go(A,Ao,lo,n if last else hi)
        go(C,Co,lo,hi)
    def end():
        go(C,Co,n-NB,n)
        for c in started: c.wait()
    return done,end


def first_kernel(g1,g2,Ao,Co,R,M,X,T,A,C,D,sem,osem):
    n=A.shape[0]
    left=lax.axis_index("tm")==0
    cps=copies([(g1.at[0:HEAD,0:n],A.at[0:HEAD]),(g1.at[:,n:n+NB],R),(g1.at[HEAD:n,0:n],A.at[HEAD:n])],sem)
    cps.append(either(left,g2,g1.at[:,0:n],C,sem.at[3]))
    for c in cps[:2]: c.wait()
    lane=lax.broadcasted_iota(jnp.int32,(1,NB),1)
    row,col=tri(n)
    def early(i,c):
        rows=pl.ds(pl.multiple_of(i*NB,NB),NB)
        A[rows,:]=A[rows,:]+jnp.where(col==row+i*NB,R[rows,64:65],0.0)
        return c
    lax.fori_loop(0,HEAD//NB,early,0)
    def ready():
        for c in cps[2:]: c.wait()
        lax.fori_loop(HEAD//NB,n//NB,early,0)
        def init(i,c):
            rows=pl.ds(pl.multiple_of(i*NB,NB),NB)
            x=R[rows,:]
            M[rows,:]=C[rows,:]+jnp.where(col==row+i*NB,x[:,65:66],0.0)
            X[rows,:]=jnp.where(lane<17,pltpu.roll(x,96,1),0.0)
            R[rows,:]=jnp.where(lane<17,x,0.0)
            return c
        lax.fori_loop(0,n//NB,init,0)
    done,end=leaving(A,C,Ao,Co,osem)
    level(A,C,R,M,X.at[0:n],T,D,ready,done)
    X[n:n+NB,:]=gram(R)
    end()


def second_kernel(d,x,ea,eb,Ao,Co,R,M,X,T,A,C,D,sem,osem):
    n=A.shape[0]
    left=lax.axis_index("tm")==0
    cps=copies([(d.at[0:HEAD],A.at[0:HEAD])],sem)
    cps.append(either(left,ea.at[0:HEAD],eb.at[0:HEAD],C.at[0:HEAD],sem.at[1]))
    cps.append(either(left,ea.at[HEAD:n],eb.at[HEAD:n],C.at[HEAD:n],sem.at[2]))
    cps+=copies([(d.at[HEAD:n],A.at[HEAD:n]),(x.at[0:n],R)],sem.at[3:5])
    for c in cps[:2]: c.wait()
    def early(i,c):
        rows=pl.ds(pl.multiple_of(i*NB,NB),NB)
        A[rows,:]=A[rows,:]+C[rows,:]
        return c
    lax.fori_loop(0,HEAD//NB,early,0)
    def ready():
        for c in cps[2:]: c.wait()
        lax.fori_loop(HEAD//NB,n//NB,early,0)
        def init(i,c):
            rows=pl.ds(pl.multiple_of(i*NB,NB),NB)
            M[rows,:]=C[rows,:]
            X[rows,:]=jnp.zeros((NB,NB),f32)
            return c
        lax.fori_loop(0,n//NB,init,0)
    done,end=leaving(A,C,Ao,Co,osem)
    level(A,C,R,M,X.at[0:n],T,D,ready,done)
    X[n:n+NB,:]=gram(R)
    end()


def back(A,T,v,x):
    n=A.shape[0]
    for j in reversed(range(n//NB)):
        rows=slice(j*NB,j*NB+NB)
        col=v[rows,0:1]
        if j*NB+NB<n:
            col=col-jnp.sum(A[rows,j*NB+NB:n]*x[:,j*NB+NB:n],axis=1,keepdims=True)
        x[:,rows]=jnp.sum(T[rows,:]*col,axis=0,keepdims=True)


def fixed(aug):
    lane=lax.broadcasted_iota(jnp.int32,(8,NB),1); sub=lax.broadcasted_iota(jnp.int32,(8,NB),0)
    g=[aug[0:8,:],aug[8:16,:]]
    drain(factor(g))
    f=jnp.zeros((1,NB),f32)
    for i in range(2):
        t=jnp.where(lane<=sub+8*i,g[i],0.0)
        f=f+jnp.sum(t*g[i][:,16:17],axis=0,keepdims=True)
    lane1=lax.broadcasted_iota(jnp.int32,(1,NB),1)
    return f,jnp.where(lane1<16,-f,jnp.where(lane1==16,1.0,0.0))


def third_kernel(m,do,xo,x1,x2,r2,a2,c2,t2,r1,a1,c1,t1,fx,O,A,Q,R,Y,T,A2,C2,T2,R2,A1,C1,T1,R1,X1,X2,D,v,x,sem):
    n=A.shape[0]
    heads=copies([(m.at[0:HEAD],A.at[0:HEAD]),(do.at[0:HEAD],Q.at[0:HEAD])],sem.at[0:2])
    rests=copies([(m.at[HEAD:n],A.at[HEAD:n]),(do.at[HEAD:n],Q.at[HEAD:n]),(xo,Y),(x2,X2),(x1.at[n:n+NB],X1)],sem.at[2:7])
    later=[pltpu.make_async_copy(s,d,sem.at[7+i]) for i,(s,d) in enumerate([(r2,R2),(a2,A2),(c2,C2),(t2,T2),(r1,R1),(a1,A1),(c1,C1),(t1,T1)])]
    for c in heads: c.wait()
    def early(i,c):
        rows=pl.ds(pl.multiple_of(i*NB,NB),NB)
        A[rows,:]=A[rows,:]+Q[rows,:]
        return c
    lax.fori_loop(0,HEAD//NB,early,0)
    def ready():
        for c in rests: c.wait()
        for c in later: c.start()
        lax.fori_loop(HEAD//NB,n//NB,early,0)
        def init(i,c):
            rows=pl.ds(pl.multiple_of(i*NB,NB),NB)
            R[rows,:]=Y[rows,:]+X2[rows,:]
            return c
        lax.fori_loop(0,n//NB,init,0)
    level(A,None,R,None,None,T,D,ready)
    f,q=fixed(fx[...]-(X1[...]+Y[n:n+NB,:]+X2[n:n+NB,:]+gram(R))[0:16,:])
    for c in later: c.wait()
    def rhs(ref):
        return jnp.sum(ref[...]*q,axis=1,keepdims=True)
    v[...]=jnp.broadcast_to(rhs(R),v.shape)
    back(A,T,v,x.at[2:3])
    v[...]=jnp.broadcast_to(rhs(R2)-jnp.sum(C2[...]*x[2:3,:],axis=1,keepdims=True),v.shape)
    back(A2,T2,v,x.at[1:2])
    v[...]=jnp.broadcast_to(rhs(R1)-jnp.sum(C1[...]*x[1:2,:],axis=1,keepdims=True),v.shape)
    back(A1,T1,v,x.at[0:1])
    x[3:4,0:NB]=f
    O[...]=x[...]


SHAPE=jax.ShapeDtypeStruct
LIMIT=60*2**20
HEAD=256


def elimination(kernel,name,n,*args):
    vm=pltpu.VMEM
    return pl.pallas_call(kernel,
        out_shape=[SHAPE((n,n),f32),SHAPE((n,n),f32),SHAPE((n,NB),f32),SHAPE((n,n),f32),SHAPE((n+NB,NB),f32),SHAPE((n,NB),f32)],
        in_specs=[pl.BlockSpec(memory_space=pl.ANY)]*len(args),
        out_specs=[pl.BlockSpec(memory_space=pl.ANY)]*2+[pl.BlockSpec(memory_space=vm)]*4,
        scratch_shapes=[vm((n,n),f32),vm((n,n),f32),vm((NB,NB),f32),pltpu.SemaphoreType.DMA((5,)),pltpu.SemaphoreType.DMA((9,))],
        compiler_params=pltpu.CompilerParams(vmem_limit_bytes=LIMIT),name=name)(*args)


def finish(n,*args):
    vm=pltpu.VMEM
    big=vm((n,n),f32); tall=vm((n,NB),f32); plus=vm((n+NB,NB),f32); one=vm((NB,NB),f32)
    return pl.pallas_call(third_kernel,out_shape=SHAPE((8,n),f32),
        in_specs=[pl.BlockSpec(memory_space=pl.ANY)]*13+[pl.BlockSpec(memory_space=vm)],out_specs=pl.BlockSpec(memory_space=vm),
        scratch_shapes=[big,big,tall,plus,tall,big,big,tall,tall,big,big,tall,tall,one,plus,one,tall,vm((8,n),f32),pltpu.SemaphoreType.DMA((15,))],
        compiler_params=pltpu.CompilerParams(vmem_limit_bytes=LIMIT),name='third')(*args)


def body(edge_prec, nugget, arrow, fixed_prec, rhs_latent, rhs_fixed):
    slab=edge_prec.shape[1]; n=edge_prec.shape[2]; k=arrow.shape[0]
    left=lax.axis_index("tm")==0
    swap=[(0,1),(1,0)]
    sign=jnp.where(left,1.0,-1.0)
    ends=lambda a: (jnp.where(left,a[0],a[1]),jnp.where(left,a[1],a[0]))
    nug_end,nug_mid=ends(nugget)
    r_end,r_mid=ends(jnp.moveaxis(jnp.concatenate([arrow,rhs_latent[None]],axis=0),0,-1))
    pad=lambda a,w: jnp.pad(a,((0,0),(0,w-a.shape[1])))
    aux=jnp.concatenate([pad(r_end*sign,32),pad(r_mid*(-sign),32),pad(jnp.stack([nug_end,nug_mid],axis=1),64)],axis=1)
    G1,G2=gather(edge_prec,aux)
    G1=G1.reshape(-1,n+NB); G2=G2.reshape(-1,n)
    E=lax.ppermute(G2,"tm",[(1,0)])
    A1,C1,R1,D1,X1,T1=elimination(first_kernel,'first',n,G1,G2)
    D_o=lax.ppermute(D1,"tm",swap); X_o=lax.ppermute(X1,"tm",swap)
    A2,C2,R2,M2,X2,T2=elimination(second_kernel,'second',n,D1,X1,E,G2)
    fx=jnp.pad(jnp.concatenate([fixed_prec,rhs_fixed[:,None]],axis=1),((0,0),(0,NB-k-1)))
    out=finish(n,M2,D_o,X_o,X1,X2,R2,A2,C2,T2,R1,A1,C1,T1,fx)
    mine=lax.dynamic_slice(out,(0,lax.axis_index("blk")*slab),(2,slab))
    end=mine[0]*sign; mid=mine[1]*(-sign)
    lat=jnp.stack([jnp.where(left,end,mid),jnp.where(left,mid,end)])
    f=out[3,:k]
    f=jnp.where(left,f,lax.ppermute(f,"tm",[(0,1)]))
    return lat,f


def solution(mesh):
    P=jax.sharding.PartitionSpec
    placed=(P("tm","blk",None),P("tm","blk"),P(None,"tm","blk"),P(),P("tm","blk"),P())
    return jax.shard_map(body,mesh=mesh,in_specs=placed,out_specs=(P("tm","blk"),P()),check_vma=False)
```

```python
import itertools
import jax, jax.numpy as jnp
from jax import lax
from jax.experimental import pallas as pl
from jax.experimental.pallas import tpu as pltpu

f32=jnp.float32; bf16=jnp.bfloat16
NB=128

def split(x):
    hi=x.astype(bf16); lo=(x-hi.astype(f32)).astype(bf16)
    return hi,lo

def dot3(a,b):
    ah,al=split(a); bh,bl=split(b)
    return jnp.dot(jnp.concatenate([ah,ah,al],axis=1),jnp.concatenate([bh,bl,bh],axis=0),preferred_element_type=f32)

def factor(G):
    n=len(G); F=(8,128)
    lane=lax.broadcasted_iota(jnp.int32,F,1); sub=lax.broadcasted_iota(jnp.int32,F,0)
    down=lambda x,s: jnp.broadcast_to(x[s:s+1,:],F)
    across=lambda x,c: jnp.broadcast_to(x[:,c:c+1],F)
    cols=[across(G[0],k) for k in range(8)]
    for j in range(n):
        g=G[j]; o=8*j
        inb=(lane>=o)&(lane<o+8)
        rows=[jnp.where(inb,jnp.where(lane==o+s,1.0,0.0),down(g,s)) for s in range(8)]
        N=[None]*8; r=[None]*8; L=[None]*8
        more=j+1<n
        if more:
            cc=[across(G[j+1],o+k) for k in range(8)]
            nc=[across(G[j+1],o+8+k) for k in range(8)]
            nxt=jnp.where(inb,0.0,G[j+1])
        for s in range(8):
            d=down(cols[s],s)
            r[s]=lax.rsqrt(d)
            N[s]=rows[s]*r[s]
            low=cols[s]*r[s]
            L[s]=[down(low,i) if i>s else None for i in range(8)]
            inv=1.0/d
            for i in range(s+1,8):
                rows[i]=rows[i]-L[s][i]*N[s]
                cols[i]=cols[i]-(cols[s]*down(cols[s],i))*inv
            if more:
                cs=cc[s]*r[s]
                nxt=nxt-cs*N[s]
                for i in range(s+1,8): cc[i]=cc[i]-L[s][i]*cs
                for k in range(8): nc[k]=nc[k]-cs*down(cs,k)
        out=N[0]
        for s in range(1,8): out=jnp.where(sub==s,N[s],out)
        G[j]=out
        if more:
            G[j+1]=nxt; cols=nc
        if j+2<n:
            Z=[None]*8
            for s in reversed(range(8)):
                v=N[s]
                for i in reversed(range(s+1,8)): v=v-L[s][i]*Z[i]
                Z[s]=v*r[s]
            near=min(n,j+4)
            for h in range(j+2,near):
                t=[across(G[h],o+k)*Z[k] for k in range(8)]
                u=((t[0]+t[1])+(t[2]+t[3]))+((t[4]+t[5])+(t[6]+t[7]))
                G[h]=jnp.where(inb,0.0,G[h])-u
            if near<n:
                z=Z[0]
                for s in range(1,8): z=jnp.where(sub==s,Z[s],z)
                zh=z.astype(bf16).astype(f32)
                def place(x):
                    x=jnp.concatenate([jnp.zeros((o,128),f32)]*(o>0)+[x]+[jnp.zeros((120-o,128),f32)]*(o<120),axis=0)
                    return x.astype(bf16)
                wh,wl=place(zh),place(z-zh)
                first=near//2*2
                lh,ll=split(jnp.concatenate(G[first:],axis=0))
                w=jnp.concatenate([jnp.concatenate([wh,wl],axis=1),jnp.concatenate([wh,jnp.zeros_like(wl)],axis=1)],axis=0)
                u=jnp.dot(jnp.concatenate([lh,ll],axis=1),w,preferred_element_type=f32)
                u=u[:,:128]+u[:,128:]
                for h in range(near,n):
                    G[h]=jnp.where(inb,0.0,G[h])-u[8*(h-first):8*(h-first)+8]
        yield

def diag_step(D,T,j):
    G=[D[8*g:8*g+8,:] for g in range(16)]
    yield from factor(G)
    row=lax.broadcasted_iota(jnp.int32,(8,128),0); col=lax.broadcasted_iota(jnp.int32,(8,128),1)
    for g in range(16):
        T[pl.ds(pl.multiple_of(j*NB+8*g,8),8),:]=jnp.where(col<=row+8*g,G[g],0.0)

def small_step(A,D,T,j):
    n=j+1
    o=pl.multiple_of(j*NB,NB); on=pl.multiple_of(n*NB,NB)
    t=T[pl.ds(o,NB),:]; x=A[pl.ds(o,NB),pl.ds(on,NB)]
    th,tl=split(t); xh,xl=split(x.T)
    y=dot3(t,x)
    yt=lax.dot_general(jnp.concatenate([xh,xh,xl],axis=1),jnp.concatenate([th,tl,th],axis=1),(((1,),(1,)),((),())),preferred_element_type=f32)
    D[...]=A[pl.ds(on,NB),pl.ds(on,NB)]-dot3(yt,y)

def bulk(A,C,R,M,Rm,t,j,low=0,ch=256):
    N=A.shape[0]
    o=pl.multiple_of(j*NB,NB)
    th,tl=split(t); tk=jnp.concatenate([th,th,tl],axis=1)
    def panel(ref,c0,w):
        x=ref[pl.ds(o,NB),c0:c0+w]
        xh,xl=split(x)
        y=jnp.dot(tk,jnp.concatenate([xh,xl,xh],axis=0),preferred_element_type=f32)
        ref[pl.ds(o,NB),c0:c0+w]=y
        yh,yl=split(y)
        return y,jnp.concatenate([yh,yl,yh],axis=0)
    def trans(y):
        h,l=split(y.T)
        return jnp.concatenate([h,h,l],axis=1)
    def upd(ref,r,c,w,lhs,rhs):
        ref[r*ch:r*ch+ch,c*ch:c*ch+w]-=jnp.dot(lhs,rhs,preferred_element_type=f32)
    nch=N//ch
    lane=lax.broadcasted_iota(jnp.int32,(1,ch),1)
    pa=[None]*nch; pc=[None]*nch; ta=[None]*nch; tc=[None]*nch
    for c in range(low,nch):
        pa[c]=panel(A,c*ch,ch); yield
    pr=panel(R,0,128); yield
    for c in range(low,nch):
        ta[c]=trans(jnp.where(lane+c*ch>=o+NB,pa[c][0],0.0)); yield
    if C is not None:
        for c in range(nch):
            pc[c]=panel(C,c*ch,ch); yield
            tc[c]=trans(pc[c][0]); yield
    for r in range(low,nch):
        for c in range(r,nch):
            upd(A,r,c,ch,ta[r],pa[c][1]); yield
        upd(R,r,0,128,ta[r],pr[1]); yield
        if C is not None:
            for c in range(nch):
                upd(C,r,c,ch,ta[r],pc[c][1]); yield
    if C is not None:
        for r in range(nch):
            for c in range(r,nch):
                upd(M,r,c,ch,tc[r],pc[c][1]); yield
            upd(Rm,r,0,128,tc[r],pr[1]); yield

def drain(g):
    for _ in g: pass

def mix(a,b,na,nb):
    done=0
    for i in range(na):
        while done<(i+1)*nb//na:
            next(b,None); done+=1
        next(a,None)
    drain(b); drain(a)

def pieces(nch,low,coupled):
    left=nch-low
    count=2*left+1+left*(left+1)//2+left
    return count+(2*nch+left*nch+nch*(nch+1)//2+nch if coupled else 0)

def level(A,C,R,M,Rm,T,D,ready=None,done=None,ch=256):
    nb=A.shape[0]//NB; nch=A.shape[0]//ch; per=ch//NB
    D[...]=A[0:NB,0:NB]
    drain(diag_step(D,T,0))
    small_step(A,D,T,0)
    if ready is not None: ready()
    def make(low):
        def body(j,c):
            t=T[pl.ds(pl.multiple_of((j-1)*NB,NB),NB),:]
            mix(diag_step(D,T,j),bulk(A,C,R,M,Rm,t,j-1,low),16,pieces(nch,low,C is not None))
            @pl.when(j<nb-1)
            def _(): small_step(A,D,T,j)
            return c
        return body
    if C is None:
        lax.fori_loop(1,nb,make(0),0)
    else:
        for low in range(nch):
            lax.fori_loop(max(1,low*per),low*per+per,make(low),0)
            done(low)
    drain(bulk(A,C,R,M,Rm,T[(nb-1)*NB:nb*NB,:],nb-1,nch))


def gram(R):
    z=R[...]
    zh,zl=split(z)
    dn=(((0,),(0,)),((),()))
    lhs=jnp.concatenate([zh,zh,zl],axis=0); rhs=jnp.concatenate([zh,zl,zh],axis=0)
    return lax.dot_general(lhs,rhs,dn,preferred_element_type=f32)


SIDE=4


def place():
    blk=lax.axis_index("blk")
    return [blk//(SIDE*SIDE),(blk//SIDE)%SIDE,blk%SIDE]


def beside(at,axis,step):
    at=list(at); at[axis]=lax.rem(at[axis]+step,SIDE)
    return {"blk":(at[0]*SIDE+at[1])*SIDE+at[2]}


def meet(others):
    barrier=pltpu.get_barrier_semaphore()
    for device in others:
        pl.semaphore_signal(barrier,inc=1,device_id=device,device_id_type=pl.DeviceIdType.MESH)
    pl.semaphore_wait(barrier,len(others))


def spread(slab,G,send,recv,local):
    at=place(); rows,lanes=slab.shape; tiles=lanes//NB
    cuts=[0]+[NB*((tiles*(q+1)+2-q)//3) for q in range(3)]; cuts[3]=lanes
    def piece(q,t,coord,part):
        order=[(q+i)%3 for i in range(3)]
        idx=list(at)
        for a in order[:t]: idx[a]=pl.ds(0,SIDE)
        idx[order[t]]=coord
        return G.at[idx[0],idx[1],idx[2],part,cuts[q]:cuts[q+1]]
    whole=pl.ds(0,rows); half=[pl.ds(0,rows//2),pl.ds(rows//2,rows//2)]
    def remote(src,dst,q,t,s,step):
        return pltpu.make_async_remote_copy(src_ref=src,dst_ref=dst,send_sem=send.at[q,t,s],recv_sem=recv.at[q,t,s],
            device_id=beside(at,(q+t)%3,step),device_id_type=pl.DeviceIdType.MESH)
    own=pltpu.make_async_copy(slab,G.at[at[0],at[1],at[2]],local)
    own.start()
    sent=[]
    for t in range(3):
        direct=t<2
        first=[]
        for q in range(3):
            dst=piece(q,t,at[(q+t)%3],whole)
            src=dst if t else slab.at[:,cuts[q]:cuts[q+1]]
            group=[remote(src,dst,q,t,s,step) for s,step in enumerate((1,3,2) if direct else (1,3))]
            for c in group: c.start()
            first.append(group)
        if t==0: own.wait()
        yield
        second=[]
        for q in range(3):
            for c in first[q]: c.wait_recv()
            if not direct:
                for d in range(2):
                    ref=piece(q,t,lax.rem(at[(q+t)%3]+(3 if d==0 else 1),SIDE),half[d])
                    c=remote(ref,ref,q,t,2+d,1 if d==0 else 3); c.start(); second.append(c)
        yield
        for c in second: c.wait_recv()
        sent+=sum(first,[])+second
    for c in sent: c.wait_send()


def neighbours():
    at=place()
    return [beside(at,axis,step) for axis in range(3) for step in (1,2,3)]


def gather_kernel(edge,aux,G1,G2,s1,s2,send,recv,local):
    n=edge.shape[2]
    left=lax.axis_index("tm")==0
    e0,e1=edge[0],edge[1]
    s1[:,0:n]=e1+jnp.where(left,e0,0.0)
    s1[:,n:n+NB]=aux[...]
    s2[...]=jnp.where(left,e1,e0)
    meet(neighbours())
    gens=[spread(s,G,send.at[i],recv.at[i],local.at[i]) for i,(s,G) in enumerate([(s1,G1),(s2,G2)])]
    for _ in itertools.zip_longest(*gens): pass


def gather(edge,aux):
    rows,n=edge.shape[1:]
    shape=lambda w: SHAPE((SIDE,SIDE,SIDE,rows,w),f32)
    sem=pltpu.SemaphoreType.DMA((2,3,3,4))
    vm=pltpu.VMEM
    return pl.pallas_call(gather_kernel,out_shape=[shape(n+NB),shape(n)],
        in_specs=[pl.BlockSpec(memory_space=vm)]*2,out_specs=[pl.BlockSpec(memory_space=pl.ANY)]*2,
        scratch_shapes=[vm((rows,n+NB),f32),vm((rows,n),f32),sem,sem,pltpu.SemaphoreType.DMA((2,))],
        compiler_params=pltpu.CompilerParams(collective_id=0,has_side_effects=True),name='gather')(edge,aux)


def either(left,a,b,dst,sem):
    @pl.when(left)
    def _(): pltpu.make_async_copy(a,dst,sem).start()
    @pl.when(jnp.logical_not(left))
    def _(): pltpu.make_async_copy(b,dst,sem).start()
    return pltpu.make_async_copy(a,dst,sem)


def copies(pairs,sem):
    out=[pltpu.make_async_copy(s,d,sem.at[i]) for i,(s,d) in enumerate(pairs)]
    for c in out: c.start()
    return out


def tri(n):
    return lax.broadcasted_iota(jnp.int32,(NB,n),0),lax.broadcasted_iota(jnp.int32,(NB,n),1)


def leaving(A,C,Ao,Co,sem):
    n=A.shape[0]; per=2
    started=[]
    def go(src,dst,lo,hi):
        c=pltpu.make_async_copy(src.at[lo:hi],dst.at[lo:hi],sem.at[len(started)])
        c.start(); started.append(c)
    def done(low):
        lo,hi=max(0,(per*low-1)*NB),(per*low+1)*NB
        last=hi+NB==n
        go(A,Ao,lo,n if last else hi)
        go(C,Co,lo,hi)
    def end():
        go(C,Co,n-NB,n)
        for c in started: c.wait()
    return done,end


def first_kernel(g1,g2,Ao,Co,R,M,X,T,A,C,D,sem,osem):
    n=A.shape[0]
    left=lax.axis_index("tm")==0
    cps=copies([(g1.at[0:HEAD,0:n],A.at[0:HEAD]),(g1.at[:,n:n+NB],R),(g1.at[HEAD:n,0:n],A.at[HEAD:n])],sem)
    cps.append(either(left,g2,g1.at[:,0:n],C,sem.at[3]))
    for c in cps[:2]: c.wait()
    lane=lax.broadcasted_iota(jnp.int32,(1,NB),1)
    row,col=tri(n)
    def early(i,c):
        rows=pl.ds(pl.multiple_of(i*NB,NB),NB)
        A[rows,:]=A[rows,:]+jnp.where(col==row+i*NB,R[rows,64:65],0.0)
        return c
    lax.fori_loop(0,HEAD//NB,early,0)
    def ready():
        for c in cps[2:]: c.wait()
        lax.fori_loop(HEAD//NB,n//NB,early,0)
        def init(i,c):
            rows=pl.ds(pl.multiple_of(i*NB,NB),NB)
            x=R[rows,:]
            M[rows,:]=C[rows,:]+jnp.where(col==row+i*NB,x[:,65:66],0.0)
            X[rows,:]=jnp.where(lane<17,pltpu.roll(x,96,1),0.0)
            R[rows,:]=jnp.where(lane<17,x,0.0)
            return c
        lax.fori_loop(0,n//NB,init,0)
    done,end=leaving(A,C,Ao,Co,osem)
    level(A,C,R,M,X.at[0:n],T,D,ready,done)
    X[n:n+NB,:]=gram(R)
    end()


def second_kernel(d,x,ea,eb,Ao,Co,R,M,X,T,A,C,D,sem,osem):
    n=A.shape[0]
    left=lax.axis_index("tm")==0
    cps=copies([(d.at[0:HEAD],A.at[0:HEAD])],sem)
    cps.append(either(left,ea.at[0:HEAD],eb.at[0:HEAD],C.at[0:HEAD],sem.at[1]))
    cps.append(either(left,ea.at[HEAD:n],eb.at[HEAD:n],C.at[HEAD:n],sem.at[2]))
    cps+=copies([(d.at[HEAD:n],A.at[HEAD:n]),(x.at[0:n],R)],sem.at[3:5])
    for c in cps[:2]: c.wait()
    def early(i,c):
        rows=pl.ds(pl.multiple_of(i*NB,NB),NB)
        A[rows,:]=A[rows,:]+C[rows,:]
        return c
    lax.fori_loop(0,HEAD//NB,early,0)
    def ready():
        for c in cps[2:]: c.wait()
        lax.fori_loop(HEAD//NB,n//NB,early,0)
        def init(i,c):
            rows=pl.ds(pl.multiple_of(i*NB,NB),NB)
            M[rows,:]=C[rows,:]
            X[rows,:]=jnp.zeros((NB,NB),f32)
            return c
        lax.fori_loop(0,n//NB,init,0)
    done,end=leaving(A,C,Ao,Co,osem)
    level(A,C,R,M,X.at[0:n],T,D,ready,done)
    X[n:n+NB,:]=gram(R)
    end()


def back(A,T,R,x,onward=()):
    n=A.shape[0]
    for j in reversed(range(n//NB)):
        rows=slice(j*NB,j*NB+NB)
        col=jnp.sum(R[rows,:],axis=1,keepdims=True)
        part=jnp.sum(T[rows,:]*col,axis=0,keepdims=True)
        x[:,rows]=part
        if j: R[0:j*NB,:]-=A[0:j*NB,rows]*part
        for C,S in onward: S[...]-=C[:,rows]*part


def fixed(aug):
    lane=lax.broadcasted_iota(jnp.int32,(8,NB),1); sub=lax.broadcasted_iota(jnp.int32,(8,NB),0)
    g=[aug[0:8,:],aug[8:16,:]]
    drain(factor(g))
    f=jnp.zeros((1,NB),f32)
    for i in range(2):
        t=jnp.where(lane<=sub+8*i,g[i],0.0)
        f=f+jnp.sum(t*g[i][:,16:17],axis=0,keepdims=True)
    lane1=lax.broadcasted_iota(jnp.int32,(1,NB),1)
    return f,jnp.where(lane1<16,-f,jnp.where(lane1==16,1.0,0.0))


def third_kernel(m,do,xo,x1,x2,r2,a2,c2,t2,r1,a1,c1,t1,fx,O,A,Q,R,Y,T,A2,C2,T2,R2,A1,C1,T1,R1,X1,X2,D,x,sem):
    n=A.shape[0]
    heads=copies([(m.at[0:HEAD],A.at[0:HEAD]),(do.at[0:HEAD],Q.at[0:HEAD])],sem.at[0:2])
    rests=copies([(m.at[HEAD:n],A.at[HEAD:n]),(do.at[HEAD:n],Q.at[HEAD:n]),(xo,Y),(x2,X2),(x1.at[n:n+NB],X1)],sem.at[2:7])
    later=[pltpu.make_async_copy(s,d,sem.at[7+i]) for i,(s,d) in enumerate([(r2,R2),(a2,A2),(c2,C2),(t2,T2),(r1,R1),(a1,A1),(c1,C1),(t1,T1)])]
    for c in heads: c.wait()
    def early(i,c):
        rows=pl.ds(pl.multiple_of(i*NB,NB),NB)
        A[rows,:]=A[rows,:]+Q[rows,:]
        return c
    lax.fori_loop(0,HEAD//NB,early,0)
    def ready():
        for c in rests: c.wait()
        for c in later: c.start()
        lax.fori_loop(HEAD//NB,n//NB,early,0)
        def init(i,c):
            rows=pl.ds(pl.multiple_of(i*NB,NB),NB)
            R[rows,:]=Y[rows,:]+X2[rows,:]
            return c
        lax.fori_loop(0,n//NB,init,0)
    level(A,None,R,None,None,T,D,ready)
    f,q=fixed(fx[...]-(X1[...]+Y[n:n+NB,:]+X2[n:n+NB,:]+gram(R))[0:16,:])
    for c in later: c.wait()
    for ref in (R,R2,R1): ref[...]=ref[...]*q
    back(A,T,R,x.at[2:3],[(C2,R2)])
    back(A2,T2,R2,x.at[1:2],[(C1,R1)])
    back(A1,T1,R1,x.at[0:1])
    x[3:4,0:NB]=f
    O[...]=x[...]


SHAPE=jax.ShapeDtypeStruct
LIMIT=60*2**20
HEAD=256


def elimination(kernel,name,n,*args):
    vm=pltpu.VMEM
    return pl.pallas_call(kernel,
        out_shape=[SHAPE((n,n),f32),SHAPE((n,n),f32),SHAPE((n,NB),f32),SHAPE((n,n),f32),SHAPE((n+NB,NB),f32),SHAPE((n,NB),f32)],
        in_specs=[pl.BlockSpec(memory_space=pl.ANY)]*len(args),
        out_specs=[pl.BlockSpec(memory_space=pl.ANY)]*2+[pl.BlockSpec(memory_space=vm)]*4,
        scratch_shapes=[vm((n,n),f32),vm((n,n),f32),vm((NB,NB),f32),pltpu.SemaphoreType.DMA((5,)),pltpu.SemaphoreType.DMA((9,))],
        compiler_params=pltpu.CompilerParams(vmem_limit_bytes=LIMIT),name=name)(*args)


def finish(n,*args):
    vm=pltpu.VMEM
    big=vm((n,n),f32); tall=vm((n,NB),f32); plus=vm((n+NB,NB),f32); one=vm((NB,NB),f32)
    return pl.pallas_call(third_kernel,out_shape=SHAPE((8,n),f32),
        in_specs=[pl.BlockSpec(memory_space=pl.ANY)]*13+[pl.BlockSpec(memory_space=vm)],out_specs=pl.BlockSpec(memory_space=vm),
        scratch_shapes=[big,big,tall,plus,tall,big,big,tall,tall,big,big,tall,tall,one,plus,one,vm((8,n),f32),pltpu.SemaphoreType.DMA((15,))],
        compiler_params=pltpu.CompilerParams(vmem_limit_bytes=LIMIT),name='third')(*args)


def body(edge_prec, nugget, arrow, fixed_prec, rhs_latent, rhs_fixed):
    slab=edge_prec.shape[1]; n=edge_prec.shape[2]; k=arrow.shape[0]
    left=lax.axis_index("tm")==0
    swap=[(0,1),(1,0)]
    sign=jnp.where(left,1.0,-1.0)
    ends=lambda a: (jnp.where(left,a[0],a[1]),jnp.where(left,a[1],a[0]))
    nug_end,nug_mid=ends(nugget)
    r_end,r_mid=ends(jnp.moveaxis(jnp.concatenate([arrow,rhs_latent[None]],axis=0),0,-1))
    pad=lambda a,w: jnp.pad(a,((0,0),(0,w-a.shape[1])))
    aux=jnp.concatenate([pad(r_end*sign,32),pad(r_mid*(-sign),32),pad(jnp.stack([nug_end,nug_mid],axis=1),64)],axis=1)
    G1,G2=gather(edge_prec,aux)
    G1=G1.reshape(-1,n+NB); G2=G2.reshape(-1,n)
    E=lax.ppermute(G2,"tm",[(1,0)])
    A1,C1,R1,D1,X1,T1=elimination(first_kernel,'first',n,G1,G2)
    D_o=lax.ppermute(D1,"tm",swap); X_o=lax.ppermute(X1,"tm",swap)
    A2,C2,R2,M2,X2,T2=elimination(second_kernel,'second',n,D1,X1,E,G2)
    fx=jnp.pad(jnp.concatenate([fixed_prec,rhs_fixed[:,None]],axis=1),((0,0),(0,NB-k-1)))
    out=finish(n,M2,D_o,X_o,X1,X2,R2,A2,C2,T2,R1,A1,C1,T1,fx)
    mine=lax.dynamic_slice(out,(0,lax.axis_index("blk")*slab),(2,slab))
    end=mine[0]*sign; mid=mine[1]*(-sign)
    lat=jnp.stack([jnp.where(left,end,mid),jnp.where(left,mid,end)])
    f=out[3,:k]
    f=jnp.where(left,f,lax.ppermute(f,"tm",[(0,1)]))
    return lat,f


def solution(mesh):
    P=jax.sharding.PartitionSpec
    placed=(P("tm","blk",None),P("tm","blk"),P(None,"tm","blk"),P(),P("tm","blk"),P())
    return jax.shard_map(body,mesh=mesh,in_specs=placed,out_specs=(P("tm","blk"),P()),check_vma=False)
```
